128 devices in a mesh: dp: 8 (over x, core), seq: 16 (over y, z).
Axes of the slice: x: 4, y: 4, z: 4, core: 2. Of those that a mesh axis runs over, the one named last changes fastest.
Arguments:
- queries: bfloat16 [8, 2048, 1024], P('dp', 'seq'), may hold values from -6 to 6
- key_vectors: bfloat16 [8, 2048, 2, 1024], P('dp', 'seq'), may hold values from -6 to 6
- values: bfloat16 [8, 2048, 2, 1024], P('dp', 'seq'), may hold values from -0.08984375 to 0.08984375
- beta_raw: float32 [8, 2048, 16], P('dp', 'seq'), may hold values from -2 to 12
- cotangent: bfloat16 [8, 2048, 2048], P('dp', 'seq'), may hold values from -6 to 6
- w_out: bfloat16 [1024, 2048], P(('dp', 'seq')), may hold values from -0.1875 to 0.1875
Outputs:
- projected: bfloat16 [8, 2048, 2048], P('dp', 'seq')
- grad_queries: bfloat16 [8, 2048, 1024], P('dp', 'seq')
- grad_keys: bfloat16 [8, 2048, 2, 1024], P('dp', 'seq')
- grad_values: bfloat16 [8, 2048, 2, 1024], P('dp', 'seq')
- grad_beta: float32 [8, 2048, 16], P('dp', 'seq')
- grad_w_out: float32 [1024, 2048], P(('dp', 'seq'))
The draws below stay inside these ranges and needn't reach their ends.
All inputs are finite; a program needn't handle non-finite values.
Results may differ from the reference program's by a relative error of at most 0.013.
Values may be sent and summed in bfloat16 or wider, within the bound.
A program may use at most 192 MiB of HBM per device.

```python
import jax
import jax.numpy as jnp
from jax import lax

D = 2048
H = 8
LOOKUP_DIM = 128
DV = 128
BLOCK = 64
SIGNAL_COUNT = 8
CLIP_COUNT = 2048


def draw_beta_raw(key, part):
    key = jax.random.fold_in(key, 11)
    key_slow, lookup_start_slot, key_high, key_low = jax.random.split(key, 4)
    slow_share = 6
    slow_low = 6.0
    slowly_varying_channels = jax.random.randint(key_slow, (SIGNAL_COUNT, 1, 1, H), 0, 10) < slow_share
    spurt_extent = LOOKUP_DIM // 4
    start_shifts = jax.random.randint(lookup_start_slot, (SIGNAL_COUNT, 3), 0, CLIP_COUNT - spurt_extent + 1)
    clip_slot = jnp.arange(CLIP_COUNT, dtype=jnp.int32)
    inside_indicator = jnp.any((clip_slot[None, :, None] >= start_shifts[:, None, :]) & (clip_slot[None, :, None] < start_shifts[:, None, :] + spurt_extent), axis=2)
    slowly_varying_entries = jax.random.uniform(key_high, (SIGNAL_COUNT, CLIP_COUNT, 2, H), jnp.float32, slow_low, 12.0)
    rapid_entries = jax.random.uniform(key_low, (SIGNAL_COUNT, CLIP_COUNT, 2, H), jnp.float32, -2.0, 2.0)
    spurt_entries = 0.25 * rapid_entries
    selected_lines = jnp.where(slowly_varying_channels, jnp.where(inside_indicator[:, :, None, None], spurt_entries, slowly_varying_entries), rapid_entries)
    return selected_lines.reshape(SIGNAL_COUNT, CLIP_COUNT, 2 * H).astype(jnp.float32)


def levels(rng, dims, shards, low, high):
    def one(dim, parts):
        draws = jax.random.uniform(jax.random.fold_in(jax.random.fold_in(rng, 6), dim), (parts,), jnp.float32, low / len(shards), high / len(shards))
        return jnp.repeat(jnp.exp(draws), dims[dim] // parts).reshape((-1,) + (1,) * (len(dims) - dim - 1))

    factor_of = one(*shards[0])
    for cut in shards[1:]:
        factor_of = factor_of * one(*cut)
    return factor_of


def gaussian(stream_key, shape, spread, reach, shards=(), held_as=jnp.bfloat16):
    gain = levels(stream_key, shape, shards, -0.22, 0.18) if shards else 1.0
    result = jax.random.normal(stream_key, shape, jnp.float32) * spread * gain
    return jnp.minimum(jnp.maximum(result, -reach), reach).astype(held_as)


def setup_inputs(seed: int = 0) -> dict:
    key_list = jax.random.split(jax.random.key(seed), 7)
    return {
        "queries": gaussian(key_list[0], (SIGNAL_COUNT, CLIP_COUNT, H * LOOKUP_DIM), 1.0, 6.0, ((0, 8), (1, 16))),
        "key_vectors": gaussian(key_list[1], (SIGNAL_COUNT, CLIP_COUNT, 2, H * LOOKUP_DIM), 1.0, 6.0, ((0, 8), (1, 16))),
        "values": gaussian(key_list[2], (SIGNAL_COUNT, CLIP_COUNT, 2, H * DV), 0.015, 0.08984375, ((0, 8), (1, 16))),
        "beta_raw": draw_beta_raw(jax.random.fold_in(key_list[6], 71), 0),
        "cotangent": gaussian(key_list[4], (SIGNAL_COUNT, CLIP_COUNT, D), 1.0, 6.0, ((0, 8), (1, 16))),
        "w_out": gaussian(key_list[5], (H * DV, D), (H * DV) ** -0.5, 0.1875, ((0, 128),)),
    }


HIGHEST_PREC = lax.Precision.HIGHEST
norm_eps = 1e-06

def block_update(carried, pieces):
    queries, key_vectors, values, betas = pieces
    step_count = key_vectors.shape[0]
    frame_count = queries.shape[0]
    key_width = key_vectors.shape[2]
    key_inner = jnp.einsum('ihd,jhd->hij', key_vectors, key_vectors, precision=HIGHEST_PREC)
    row_index = lax.broadcasted_iota(jnp.int32, (step_count, step_count), 0)
    col_index = lax.broadcasted_iota(jnp.int32, (step_count, step_count), 1)
    below_diag = (col_index < row_index).astype(jnp.float32)
    beta_heads = jnp.transpose(betas)
    system = jnp.eye(step_count, dtype=jnp.float32) + below_diag * beta_heads[:, :, None] * key_inner
    stacked = jnp.concatenate([jnp.transpose(key_vectors, (1, 0, 2)), jnp.transpose(values, (1, 0, 2))], axis=2)
    solved = jax.scipy.linalg.solve_triangular(system, beta_heads[:, :, None] * stacked, lower=True, unit_diagonal=True)
    deltas = solved[:, :, key_width:] - jnp.einsum('hid,hde->hie', solved[:, :, :key_width], carried, precision=HIGHEST_PREC)
    scores = jnp.einsum('fhd,jhd->hfj', queries, key_vectors, precision=HIGHEST_PREC)
    frame_index = lax.broadcasted_iota(jnp.int32, (frame_count, step_count), 0)
    step_index = lax.broadcasted_iota(jnp.int32, (frame_count, step_count), 1)
    visible = (step_index // 2 <= frame_index).astype(jnp.float32)
    outputs = jnp.einsum('fhd,hde->fhe', queries, carried, precision=HIGHEST_PREC)
    outputs = outputs + jnp.einsum('hfj,hje->fhe', scores * visible[None], deltas, precision=HIGHEST_PREC)
    carried = carried + jnp.einsum('jhd,hje->hde', key_vectors, deltas, precision=HIGHEST_PREC)
    return (carried, outputs)

def run_blocks(queries, key_vectors, values, betas, carried):
    frame_count, head_count, key_width = queries.shape
    block_count = frame_count // BLOCK
    grouped = (queries.reshape(block_count, BLOCK, head_count, key_width), key_vectors.reshape(block_count, 2 * BLOCK, head_count, key_width), values.reshape(block_count, 2 * BLOCK, head_count, values.shape[2]), betas.reshape(block_count, 2 * BLOCK, head_count))
    carried, outputs = lax.scan(block_update, carried, grouped)
    return (outputs.reshape(frame_count, head_count, values.shape[2]), carried)

def prepare(queries, key_vectors, values, beta_raw):
    frame_count = queries.shape[0]
    head_count = queries.shape[1] // LOOKUP_DIM
    query_heads = queries.astype(jnp.float32).reshape(frame_count, head_count, LOOKUP_DIM)
    key_heads = key_vectors.astype(jnp.float32).reshape(2 * frame_count, head_count, LOOKUP_DIM)
    key_heads = key_heads * lax.rsqrt(lax.optimization_barrier(jnp.sum(key_heads * key_heads, axis=2, keepdims=True)) + norm_eps)
    value_heads = values.astype(jnp.float32).reshape(2 * frame_count, head_count, DV)
    betas = 2.0 * jax.nn.sigmoid(beta_raw.reshape(2 * frame_count, head_count))
    return (query_heads, key_heads, value_heads, betas)

def reference(queries, key_vectors, values, beta_raw, cotangent, w_out):
    head_count = queries.shape[2] // LOOKUP_DIM

    def recurrence(query_one, key_one, value_one, raw_one):
        query_heads, key_heads, value_heads, betas = prepare(query_one, key_one, value_one, raw_one)
        start_state = jnp.zeros((head_count, LOOKUP_DIM, DV), jnp.float32)
        outputs, final_state = run_blocks(query_heads, key_heads, value_heads, betas, start_state)
        return outputs.reshape(outputs.shape[0], head_count * DV)

    def one_stream(inputs):
        query_one, key_one, value_one, raw_one, cot_one = inputs
        mixed, pullback = jax.vjp(recurrence, query_one, key_one, value_one, raw_one)
        mixed_bf = mixed.astype(jnp.bfloat16)
        projected = jnp.dot(mixed_bf.astype(jnp.float32), w_out.astype(jnp.float32), preferred_element_type=jnp.float32).astype(jnp.bfloat16)
        mixed_grad = lax.dot_general(cot_one.astype(jnp.float32), w_out.astype(jnp.float32), (((1,), (1,)), ((), ())), preferred_element_type=jnp.float32)
        grad_query, grad_key, grad_value, grad_raw = pullback(mixed_grad)
        weight_part = lax.dot_general(mixed_bf.astype(jnp.float32), cot_one.astype(jnp.float32), (((0,), (0,)), ((), ())), preferred_element_type=jnp.float32)
        return (projected, grad_query, grad_key, grad_value, grad_raw, weight_part)
    results = lax.map(one_stream, (queries, key_vectors, values, beta_raw, cotangent))
    return (results[0], results[1], results[2], results[3], results[4], lax.optimization_barrier(jnp.sum(results[5], axis=0)))
```

```python
import jax
import jax.numpy as jnp
from jax import lax
from jax.experimental import pallas as pl
from jax.experimental.pallas import tpu as pltpu
from jax.sharding import PartitionSpec as P

f32, bf16 = jnp.float32, jnp.bfloat16
MESH = pl.DeviceIdType.MESH
NORM_EPS = 1e-06
HEADS = 8
DIM = 128
HALF = 64
FRAMES = 128
STEPS = 256
MODEL = 2048
FEATURES = HEADS * DIM
SEQ = 16
SIDE = 4
COLS = 512


def mm(a, b, ca=1, cb=0):
    return lax.dot_general(a, b, (((ca,), (cb,)), ((), ())), preferred_element_type=f32)


def split(x):
    high = x.astype(bf16)
    return high, (x - high.astype(f32)).astype(bf16)


def mm2(a, b, ca=1, cb=0):
    return mm(a[0], b, ca, cb) + mm(a[1], b, ca, cb)


def mm3(a, b, ca=1, cb=0):
    return mm(a[0], b[0], ca, cb) + (mm(a[0], b[1], ca, cb) + mm(a[1], b[0], ca, cb))


def iota(shape, axis):
    return lax.broadcasted_iota(jnp.int32, shape, axis)


def unit_lower_inverse(blocks):
    shape = blocks[0].shape
    rows, columns = iota(shape, 0), iota(shape, 1)
    differing = rows ^ columns
    eye = (rows == columns).astype(f32)
    inverses = [eye - jnp.where(differing == 1, low, 0.0) for low in blocks]
    size = 2
    while size < shape[0]:
        mask = (differing >= size) & (differing < 2 * size)
        parts = [split(inverse) for inverse in inverses]
        offs = [split(jnp.where(mask, low, 0.0)) for low in blocks]
        firsts = [split(mm3(part, off)) for part, off in zip(parts, offs)]
        inverses = [inv - mm3(first, part) for inv, first, part in zip(inverses, firsts, parts)]
        size *= 2
    return inverses


def pick_column(array, head):
    return jnp.sum(jnp.where(iota(array.shape, 1) == head, array, 0.0), axis=1, keepdims=True)


def row_scale(keys):
    wide = keys.astype(f32)
    return lax.rsqrt(jnp.sum(wide * wide, axis=1, keepdims=True) + NORM_EPS)


def local_forward(heads):
    lows, scales = [], []
    for queries, keys, values, raw_col, raw_row in heads:
        inner = mm(keys, keys, 1, 1)
        rows, columns = iota(inner.shape, 0), iota(inner.shape, 1)
        squares = jnp.sum(jnp.where(rows == columns, inner, 0.0), axis=0, keepdims=True)
        r_row = lax.rsqrt(squares + NORM_EPS)
        r_col = row_scale(keys)
        b_col, b_row = 2.0 * jax.nn.sigmoid(raw_col), 2.0 * jax.nn.sigmoid(raw_row)
        lows.append(jnp.where(columns < rows, inner * (b_col * r_col) * r_row, 0.0))
        scales.append((r_col, r_row, b_col, b_row))
    blocks = []
    for low in lows:
        blocks += [low[:DIM, :DIM], low[DIM:, DIM:]]
    inverses = unit_lower_inverse(blocks)
    results = []
    for index, (queries, keys, values, raw_col, raw_row) in enumerate(heads):
        r_col, r_row, b_col, b_row = scales[index]
        upper, lower = inverses[2 * index], inverses[2 * index + 1]
        corner = mm3(split(lower), split(mm3(split(lows[index][DIM:, :DIM]), split(upper))))
        inverse = jnp.concatenate(
            [
                jnp.concatenate([upper, jnp.zeros_like(upper)], axis=1),
                jnp.concatenate([-corner, lower], axis=1),
            ],
            axis=0,
        )
        written = inverse * b_row
        erase = mm2(split(written * r_row), keys)
        insert = mm2(split(written), values)
        key_back = mm2(split(inverse * r_col), keys, 0, 0)
        scores = mm(queries, keys, 1, 1) * r_row
        frame, step = iota(scores.shape, 0), iota(scores.shape, 1)
        scores = jnp.where(step <= 2 * frame + 1, scores, 0.0)
        score_back = mm3(split(inverse), split(scores), 0, 1)
        eye = (iota((DIM, DIM), 0) == iota((DIM, DIM), 1)).astype(f32)
        erase_scaled = split(erase * r_col)
        transit = eye - (mm(keys, erase_scaled[0], 0, 0) + mm(keys, erase_scaled[1], 0, 0))
        back_scaled = split(key_back * b_col)
        offset = mm(values, back_scaled[0], 0, 0) + mm(values, back_scaled[1], 0, 0)
        weighted = score_back * b_col
        reads = queries.astype(f32) - mm2(split(weighted * r_col), keys, 0, 0)
        mixed = mm2(split(weighted), values, 0, 0)
        results.append((erase, insert, key_back, score_back, transit, offset, reads, mixed, r_row))
    return results


def kernel(
    q_ref, k_ref, v_ref, bcol_ref, brow_ref, cot_ref, w_ref,
    proj_ref, gq_ref, gk_ref, gv_ref, gb_ref, gw_ref,
    wg, wf, cotg, erase_s, insert_s, kback_s, sback_s, reads_s, mixed_s, rrow_s, gm_s, y_s,
    t_send, o_send, z_send, t_recv, o_recv, z_recv,
    s_send, d_send, s_recv, d_recv, mb_send, mb_full, mb_recv, gwp, gwr, gws, gwb,
    w_ss, w_rs, c_ss, c_rs, t_ss, t_rs, o_ss, o_rs, z_ss, z_rs, s_ss, s_rs, d_ss, d_rs,
    m_ss, m_rs, g_ss, g_rs, b_ss, b_rs,
):
    dp, me = lax.axis_index("dp"), lax.axis_index("seq")
    x, c = dp // 2, dp % 2
    y, z = me // SIDE, me % SIDE
    twin = x * 2 + (1 - c)

    def x_peer(step):
        return ((x + step) % SIDE) * 2 + c, me

    def y_peer(step):
        return dp, ((y + step) % SIDE) * SIDE + z

    def z_peer(step):
        return dp, y * SIDE + (z + step) % SIDE

    barrier = pltpu.get_barrier_semaphore()
    for step in range(1, SEQ):
        pl.semaphore_signal(barrier, inc=1, device_id=(dp, (me + step) % SEQ), device_id_type=MESH)
    for step in range(1, SIDE):
        pl.semaphore_signal(barrier, inc=1, device_id=x_peer(step), device_id_type=MESH)
    pl.semaphore_signal(barrier, inc=1, device_id=(twin, me), device_id_type=MESH)
    pl.semaphore_wait(barrier, SEQ - 1 + SIDE - 1 + 1)

    def remote(source, target, send_sem, recv_sem, device):
        return pltpu.make_async_remote_copy(
            src_ref=source, dst_ref=target, send_sem=send_sem, recv_sem=recv_sem,
            device_id=device, device_id_type=MESH,
        )

    def arrival(target, send_sem, recv_sem):
        remote(target, target, send_sem, recv_sem, (twin, me)).wait_recv()

    left, right = pl.ds(0, COLS), pl.ds(COLS, COLS)

    def w_copy(phase, step):
        if phase == 0:
            return wg.at[x, c, y, z], wg.at[(x - step + SIDE) % SIDE, c, y, z], x_peer(step)
        if phase == 1:
            return wg.at[:, c, y, z, :, left], wg.at[:, c, (y - step + SIDE) % SIDE, z, :, left], y_peer(step)
        if phase == 2:
            return wg.at[:, c, y, z, :, right], wg.at[:, c, y, (z - step + SIDE) % SIDE, :, right], z_peer(step)
        if phase == 3:
            return wg.at[:, c, :, z, :, left], wg.at[:, c, :, (z - step + SIDE) % SIDE, :, left], z_peer(step)
        if phase == 4:
            return wg.at[:, c, y, :, :, right], wg.at[:, c, (y - step + SIDE) % SIDE, :, :, right], y_peer(step)
        part = left if step == 1 else right
        return wg.at[:, c, :, :, :, part], wg.at[:, 1 - c, :, :, :, part], (twin, me)

    def w_steps(phase):
        return range(1, 3) if phase == 5 else range(1, SIDE)

    def w_start(phase):
        for step in w_steps(phase):
            source, _, device = w_copy(phase, step)
            sem = 3 * phase + step - 1
            remote(source, source, w_ss.at[sem], w_rs.at[sem], device).start()

    def w_arrive(phase):
        for step in w_steps(phase):
            _, target, _ = w_copy(phase, step)
            sem = 3 * phase + step - 1
            arrival(target, w_ss.at[sem], w_rs.at[sem])

    def w_sent(phase):
        for step in w_steps(phase):
            source, _, device = w_copy(phase, step)
            sem = 3 * phase + step - 1
            remote(source, source, w_ss.at[sem], w_rs.at[sem], device).wait_send()

    wg[x, c, y, z] = w_ref[...]
    w_start(0)

    def cot_copy(step):
        return remote(cot_ref, cotg.at[x], c_ss.at[step - 1], c_rs.at[step - 1], x_peer(step))

    for step in range(1, SIDE):
        cot_copy(step).start()
    cotg[x] = cot_ref[...]

    def head_lanes(head):
        return pl.ds(pl.multiple_of(head * DIM, DIM), DIM)

    def state_copies(head, half):
        owner = 2 * head + half
        rows = pl.ds(half * HALF, HALF)
        return (
            remote(t_send.at[head], t_recv.at[me], t_ss.at[owner], t_rs.at[me], (dp, owner)),
            remote(o_send.at[head, rows], o_recv.at[me], o_ss.at[owner], o_rs.at[me], (dp, owner)),
        )

    def adjoint_copy(head, half):
        owner = 2 * head + half
        rows = pl.ds(half * HALF, HALF)
        return remote(z_send.at[head, rows], z_recv.at[me], z_ss.at[owner], z_rs.at[me], (dp, owner))

    def forward_pair(index, carry):
        pair = (index + y) % SIDE
        heads = []
        for inner in range(2):
            head = 2 * pair + inner
            heads.append(
                (
                    q_ref[:, head_lanes(head)],
                    k_ref[:, head_lanes(head)],
                    v_ref[:, head_lanes(head)],
                    pick_column(bcol_ref[...], head),
                    brow_ref[head],
                )
            )
        for inner, result in enumerate(local_forward(heads)):
            head = 2 * pair + inner
            erase, insert, key_back, score_back, transit, offset, reads, mixed, r_row = result
            t_send[head] = transit
            o_send[head] = offset
            for half in range(2):
                owner = 2 * head + half

                @pl.when(owner != me)
                def _():
                    for copy in state_copies(head, half):
                        copy.start()

                @pl.when(owner == me)
                def _():
                    t_recv[me] = transit
                    o_recv[me] = offset[half * HALF : (half + 1) * HALF]

            erase_s[0, head], erase_s[1, head] = split(erase)
            insert_s[head] = insert
            kback_s[0, head], kback_s[1, head] = split(key_back)
            sback_s[0, head], sback_s[1, head] = split(score_back)
            reads_s[head] = reads.astype(bf16)
            mixed_s[head] = mixed
            rrow_s[head] = r_row

        @pl.when(index == 0)
        def _():
            w_arrive(0)
            w_start(1)
            w_start(2)

        @pl.when(index == 1)
        def _():
            w_arrive(1)
            w_start(3)
            w_arrive(2)
            w_start(4)

        return carry

    lax.fori_loop(0, HEADS // 2, forward_pair, 0)
    w_arrive(3)
    w_arrive(4)
    w_start(5)

    for step in range(1, SEQ):
        source = (me + step) % SEQ
        arrival(t_recv.at[source], t_ss.at[source], t_rs.at[source])
        arrival(o_recv.at[source], o_ss.at[source], o_rs.at[source])

    def send_state(buffer, target, value, segment, send_sems, recv_sems):
        buffer[segment] = value.astype(bf16)

        @pl.when(segment != me)
        def _():
            remote(
                buffer.at[segment], target.at[me], send_sems.at[segment], recv_sems.at[me], (dp, segment)
            ).start()

        @pl.when(segment == me)
        def _():
            target[me] = value.astype(bf16)

    def carry_state(segment, state):
        send_state(s_send, s_recv, state, segment, s_ss, s_rs)
        return mm3(split(state), split(t_recv[segment]), 1, 1) + o_recv[segment]

    last_state = lax.fori_loop(0, SEQ - 1, carry_state, jnp.zeros((HALF, DIM), f32))
    send_state(s_send, s_recv, last_state, SEQ - 1, s_ss, s_rs)

    def order_rows(core):
        def one(index, carry):
            across, block = index // 8, index % 8
            row, column = block // 2, 2 * (block % 2)
            first = wg[across, core, row, column].astype(f32)
            second = wg[across, core, row, column + 1].astype(f32)
            start = pl.multiple_of(((across * 2 + core) * 8 + block) * 16, 16)
            top = jnp.concatenate([first[:8], second[:8]], axis=0)
            bottom = jnp.concatenate([first[8:], second[8:]], axis=0)
            wf[pl.ds(start, 16), pl.ds(0, MODEL // 2)] = top.astype(bf16)
            wf[pl.ds(start, 16), pl.ds(MODEL // 2, MODEL // 2)] = bottom.astype(bf16)
            return carry

        lax.fori_loop(0, 32, one, 0)

    order_rows(c)
    w_arrive(5)
    order_rows(1 - c)

    def gradient_pair(index, carry):
        pair = (index + y) % SIDE
        rows = wf[pl.ds(pl.multiple_of(pair * 2 * DIM, 2 * DIM), 2 * DIM), :]
        both = mm(cot_ref[...], rows, 1, 1).astype(bf16)
        for inner in range(2):
            head = 2 * pair + inner
            grad = both[:, inner * DIM : (inner + 1) * DIM]
            gm_s[head] = grad
            adjoint = mm(grad, reads_s[head], 0, 0).astype(bf16)
            z_send[head] = adjoint
            for half in range(2):
                owner = 2 * head + half

                @pl.when(owner != me)
                def _():
                    adjoint_copy(head, half).start()

                @pl.when(owner == me)
                def _():
                    z_recv[me] = adjoint[half * HALF : (half + 1) * HALF]

        return carry

    lax.fori_loop(0, HEADS // 2, gradient_pair, 0)

    def early_gradient(head, carry):
        y_s[head] = mm2((sback_s[0, head], sback_s[1, head]), gm_s[head])
        return carry

    lax.fori_loop(0, HEADS, early_gradient, 0)

    for step in range(1, SEQ):
        source = (me + step) % SEQ
        arrival(s_recv.at[source], s_ss.at[source], s_rs.at[source])

    def head_state(buffer, head):
        return jnp.concatenate([buffer[2 * head], buffer[2 * head + 1]], axis=0)

    def mix_head(head, carry):
        mixed = (mm(reads_s[head], head_state(s_recv, head), 1, 1) + mixed_s[head]).astype(bf16)
        mb_send[head] = mixed
        mb_full[:, head_lanes(head)] = mixed
        return carry

    lax.fori_loop(0, HEADS, mix_head, 0)

    def mixed_copy(step):
        to = (x + step) % SIDE
        return remote(
            mb_send.at[pl.ds(2 * to, 2)], mb_recv.at[:, x], m_ss.at[step - 1], m_rs.at[step - 1], x_peer(step)
        )

    for step in range(1, SIDE):
        mixed_copy(step).start()
    mb_recv[0, x] = mb_send[2 * x]
    mb_recv[1, x] = mb_send[2 * x + 1]

    for step in range(1, SEQ):
        source = (me + step) % SEQ
        arrival(z_recv.at[source], z_ss.at[source], z_rs.at[source])

    def carry_adjoint(index, state):
        segment = SEQ - 1 - index
        send_state(d_send, d_recv, state, segment, d_ss, d_rs)
        return mm3(split(state), split(t_recv[segment])) + z_recv[segment].astype(f32)

    first_adjoint = lax.fori_loop(0, SEQ - 1, carry_adjoint, jnp.zeros((HALF, DIM), f32))
    send_state(d_send, d_recv, first_adjoint, 0, d_ss, d_rs)

    def project(index, carry):
        lanes = pl.ds(pl.multiple_of(index * COLS, COLS), COLS)
        proj_ref[:, lanes] = mm(mb_full[...], wf[:, lanes]).astype(bf16)
        return carry

    lax.fori_loop(0, MODEL // COLS, project, 0)

    for step in range(1, SIDE):
        source = (x - step + SIDE) % SIDE
        arrival(cotg.at[source], c_ss.at[step - 1], c_rs.at[step - 1])
        arrival(mb_recv.at[:, source], m_ss.at[step - 1], m_rs.at[step - 1])

    def weight_part(inner):
        mixed = mb_recv[inner].reshape(SIDE * FRAMES, DIM)

        def one(index, carry):
            lanes = pl.ds(pl.multiple_of(index * COLS, COLS), COLS)
            cot = cotg[:, :, lanes].reshape(SIDE * FRAMES, COLS)
            gwp[inner, :, lanes] = mm(mixed, cot, 0, 0)
            return carry

        lax.fori_loop(0, MODEL // COLS, one, 0)

    weight_part(1 - c)
    weight_copy = remote(gwp.at[1 - c], gwr, g_ss.at[0], g_rs.at[0], (twin, me))
    weight_copy.start()
    weight_part(c)

    for step in range(1, SEQ):
        source = (me + step) % SEQ
        arrival(d_recv.at[source], d_ss.at[source], d_rs.at[source])

    def block_copy(step):
        to = (me + step) % SEQ
        return remote(gws.at[to], gwb.at[me], b_ss.at[to], b_rs.at[me], (dp, to))

    def backward_head(head, raw_all):
        queries, keys = q_ref[:, head_lanes(head)], k_ref[:, head_lanes(head)]
        raw = pick_column(raw_all, head)
        b_col = 2.0 * jax.nn.sigmoid(raw)
        r_col, r_row = row_scale(keys), rrow_s[head]
        state, later = head_state(s_recv, head), head_state(d_recv, head)
        grad = gm_s[head]
        delta = insert_s[head] - mm2((erase_s[0, head], erase_s[1, head]), state, 1, 1)
        solved = y_s[head] + mm2((kback_s[0, head], kback_s[1, head]), later, 1, 1)
        scaled = b_col * solved
        gv_ref[:, head_lanes(head)] = scaled.astype(bf16)
        raw_grad = jnp.sum(solved * delta, axis=1, keepdims=True) * jax.nn.sigmoid(-raw)
        delta_parts, scaled_parts = split(delta), split(-scaled)
        score_grad = mm(grad, delta_parts[0], 1, 1) + mm(grad, delta_parts[1], 1, 1)
        frame, step = iota(score_grad.shape, 0), iota(score_grad.shape, 1)
        score_grad = jnp.where(step <= 2 * frame + 1, score_grad, 0.0)
        inner_grad = mm3(scaled_parts, delta_parts, 1, 1)
        row, column = iota(inner_grad.shape, 0), iota(inner_grad.shape, 1)
        inner_grad = jnp.where(column < row, inner_grad, 0.0)
        query_grad = mm(grad, state) + mm((score_grad * r_row).astype(bf16), keys)
        gq_ref[:, head_lanes(head)] = query_grad.astype(bf16)
        key_grad = mm(scaled_parts[0], state) + mm(delta_parts[0], later)
        key_grad = key_grad + mm(score_grad.astype(bf16), queries, 0, 0)
        key_grad = key_grad + mm((inner_grad * r_row).astype(bf16), keys)
        key_grad = key_grad + mm((inner_grad * r_col).astype(bf16), keys, 0, 0)
        unit = keys.astype(f32) * r_col
        along = jnp.sum(key_grad * unit, axis=1, keepdims=True)
        gk_ref[:, head_lanes(head)] = (r_col * (key_grad - unit * along)).astype(bf16)
        return raw_grad

    lane = iota((STEPS, HEADS), 1)

    def backward_pair(index, total):
        raw_all = bcol_ref[...]
        for inner in range(2):
            head = 2 * index + inner
            total = total + jnp.where(lane == head, backward_head(head, raw_all), 0.0)

        @pl.when(index == 0)
        def _():
            arrival(gwr, g_ss.at[0], g_rs.at[0])

            def one(block, carry):
                rows = pl.ds(pl.multiple_of(block * 8, 8), 8)
                gws[block] = gwp[c, rows] + gwr[rows]
                return carry

            lax.fori_loop(0, SEQ, one, 0)
            for step in range(1, SEQ):
                block_copy(step).start()
            gwb[me] = gws[me]

        return total

    gb_ref[...] = lax.fori_loop(0, HEADS // 2, backward_pair, jnp.zeros((STEPS, HEADS), f32))

    for step in range(1, SEQ):
        source = (me + step) % SEQ
        arrival(gwb.at[source], b_ss.at[source], b_rs.at[source])
    total = gwb[0]
    for block in range(1, SEQ):
        total = total + gwb[block]
    gw_ref[...] = total

    for phase in range(6):
        w_sent(phase)
    for step in range(1, SIDE):
        cot_copy(step).wait_send()
        mixed_copy(step).wait_send()
    weight_copy.wait_send()
    for step in range(1, SEQ):
        other = (me + step) % SEQ
        block_copy(step).wait_send()
        remote(t_send.at[other // 2], t_recv.at[me], t_ss.at[other], t_rs.at[me], (dp, other)).wait_send()
        half_rows = pl.ds(pl.multiple_of((other % 2) * HALF, HALF), HALF)
        remote(
            o_send.at[other // 2, half_rows], o_recv.at[me], o_ss.at[other], o_rs.at[me], (dp, other)
        ).wait_send()
        remote(
            z_send.at[other // 2, half_rows], z_recv.at[me], z_ss.at[other], z_rs.at[me], (dp, other)
        ).wait_send()
        remote(s_send.at[other], s_recv.at[me], s_ss.at[other], s_rs.at[me], (dp, other)).wait_send()
        remote(d_send.at[other], d_recv.at[me], d_ss.at[other], d_rs.at[me], (dp, other)).wait_send()


def per_device(queries, key_vectors, values, beta_raw, cotangent, w_out):
    raw_col = beta_raw.reshape(STEPS, HEADS)
    raw_row = jnp.transpose(raw_col).reshape(HEADS, 1, STEPS)
    w_rows = w_out.reshape(8, 2, MODEL // 2).transpose(1, 0, 2).reshape(16, MODEL // 2)
    vmem = pl.BlockSpec(memory_space=pltpu.VMEM)
    dma = pltpu.SemaphoreType.DMA
    out = pl.pallas_call(
        kernel,
        out_shape=(
            jax.ShapeDtypeStruct((FRAMES, MODEL), bf16),
            jax.ShapeDtypeStruct((FRAMES, FEATURES), bf16),
            jax.ShapeDtypeStruct((STEPS, FEATURES), bf16),
            jax.ShapeDtypeStruct((STEPS, FEATURES), bf16),
            jax.ShapeDtypeStruct((STEPS, HEADS), f32),
            jax.ShapeDtypeStruct((8, MODEL), f32),
        ),
        in_specs=[vmem] * 7,
        out_specs=[vmem] * 6,
        scratch_shapes=[
            pltpu.VMEM((SIDE, 2, SIDE, SIDE, 16, MODEL // 2), bf16),
            pltpu.VMEM((FEATURES, MODEL), bf16),
            pltpu.VMEM((SIDE, FRAMES, MODEL), bf16),
            pltpu.VMEM((2, HEADS, STEPS, DIM), bf16),
            pltpu.VMEM((HEADS, STEPS, DIM), f32),
            pltpu.VMEM((2, HEADS, STEPS, DIM), bf16),
            pltpu.VMEM((2, HEADS, STEPS, DIM), bf16),
            pltpu.VMEM((HEADS, FRAMES, DIM), bf16),
            pltpu.VMEM((HEADS, FRAMES, DIM), f32),
            pltpu.VMEM((HEADS, 1, STEPS), f32),
            pltpu.VMEM((HEADS, FRAMES, DIM), bf16),
            pltpu.VMEM((HEADS, STEPS, DIM), f32),
            pltpu.VMEM((HEADS, DIM, DIM), f32),
            pltpu.VMEM((HEADS, DIM, DIM), f32),
            pltpu.VMEM((HEADS, DIM, DIM), bf16),
            pltpu.VMEM((SEQ, DIM, DIM), f32),
            pltpu.VMEM((SEQ, HALF, DIM), f32),
            pltpu.VMEM((SEQ, HALF, DIM), bf16),
            pltpu.VMEM((SEQ, HALF, DIM), bf16),
            pltpu.VMEM((SEQ, HALF, DIM), bf16),
            pltpu.VMEM((SEQ, HALF, DIM), bf16),
            pltpu.VMEM((SEQ, HALF, DIM), bf16),
            pltpu.VMEM((HEADS, FRAMES, DIM), bf16),
            pltpu.VMEM((FRAMES, FEATURES), bf16),
            pltpu.VMEM((2, SIDE, FRAMES, DIM), bf16),
            pltpu.VMEM((2, DIM, MODEL), f32),
            pltpu.VMEM((DIM, MODEL), f32),
            pltpu.VMEM((SEQ, 8, MODEL), f32),
            pltpu.VMEM((SEQ, 8, MODEL), f32),
            dma((18,)), dma((18,)), dma((3,)), dma((3,)),
            dma((SEQ,)), dma((SEQ,)), dma((SEQ,)), dma((SEQ,)), dma((SEQ,)), dma((SEQ,)),
            dma((SEQ,)), dma((SEQ,)), dma((SEQ,)), dma((SEQ,)),
            dma((3,)), dma((3,)), dma((1,)), dma((1,)), dma((SEQ,)), dma((SEQ,)),
        ],
        compiler_params=pltpu.CompilerParams(
            collective_id=0, has_side_effects=True, vmem_limit_bytes=60 * 1024 * 1024
        ),
        name="delta_product",
    )(
        queries[0],
        key_vectors[0].reshape(STEPS, FEATURES),
        values[0].reshape(STEPS, FEATURES),
        raw_col,
        raw_row,
        cotangent[0],
        w_rows,
    )
    projected, grad_query, grad_key, grad_value, grad_raw, grad_weight = out
    return (
        projected[None],
        grad_query[None],
        grad_key.reshape(1, FRAMES, 2, FEATURES),
        grad_value.reshape(1, FRAMES, 2, FEATURES),
        grad_raw.reshape(1, FRAMES, 2 * HEADS),
        grad_weight,
    )


def solution(mesh):
    in_specs = (
        P("dp", "seq", None),
        P("dp", "seq", None, None),
        P("dp", "seq", None, None),
        P("dp", "seq", None),
        P("dp", "seq", None),
        P(("dp", "seq"), None),
    )
    out_specs = (
        P("dp", "seq", None),
        P("dp", "seq", None),
        P("dp", "seq", None, None),
        P("dp", "seq", None, None),
        P("dp", "seq", None),
        P(("dp", "seq"), None),
    )
    return jax.shard_map(
        per_device, mesh=mesh, in_specs=in_specs, out_specs=out_specs, check_vma=False
    )
```

```python
import jax
import jax.numpy as jnp
from jax import lax
from jax.experimental import pallas as pl
from jax.experimental.pallas import tpu as pltpu
from jax.sharding import PartitionSpec as P

f32, bf16 = jnp.float32, jnp.bfloat16
MESH = pl.DeviceIdType.MESH
NORM_EPS = 1e-06
HEADS = 8
DIM = 128
HALF = 64
FRAMES = 128
STEPS = 256
MODEL = 2048
FEATURES = HEADS * DIM
SEQ = 16
SIDE = 4
COLS = 512
W_AT = 1
RELAY_AT = 3


def mm(a, b, ca=1, cb=0):
    return lax.dot_general(a, b, (((ca,), (cb,)), ((), ())), preferred_element_type=f32)


def split(x):
    high = x.astype(bf16)
    return high, (x - high.astype(f32)).astype(bf16)


def mm2(a, b, ca=1, cb=0):
    return mm(a[0], b, ca, cb) + mm(a[1], b, ca, cb)


def mm3(a, b, ca=1, cb=0):
    return mm(a[0], b[0], ca, cb) + (mm(a[0], b[1], ca, cb) + mm(a[1], b[0], ca, cb))


def thirds(x):
    high = x.astype(bf16)
    rest = x - high.astype(f32)
    middle = rest.astype(bf16)
    return high, middle, (rest - middle.astype(f32)).astype(bf16)


def iota(shape, axis):
    return lax.broadcasted_iota(jnp.int32, shape, axis)


def unit_lower_inverse(blocks):
    shape = blocks[0].shape
    rows, columns = iota(shape, 0), iota(shape, 1)
    differing = rows ^ columns
    eye = (rows == columns).astype(f32)
    inverses = [eye - jnp.where(differing == 1, low, 0.0) for low in blocks]
    size = 2
    while size < shape[0]:
        mask = (differing >= size) & (differing < 2 * size)
        parts = [split(inverse) for inverse in inverses]
        offs = [split(jnp.where(mask, low, 0.0)) for low in blocks]
        firsts = [split(mm3(part, off)) for part, off in zip(parts, offs)]
        inverses = [inv - mm3(first, part) for inv, first, part in zip(inverses, firsts, parts)]
        size *= 2
    return inverses


def pick_column(array, head):
    return jnp.sum(jnp.where(iota(array.shape, 1) == head, array, 0.0), axis=1, keepdims=True)


def row_scale(keys):
    wide = keys.astype(f32)
    return lax.rsqrt(jnp.sum(wide * wide, axis=1, keepdims=True) + NORM_EPS)


def local_forward(heads):
    lows, scales = [], []
    for queries, keys, values, raw_col, raw_row in heads:
        inner = mm(keys, keys, 1, 1)
        rows, columns = iota(inner.shape, 0), iota(inner.shape, 1)
        squares = jnp.sum(jnp.where(rows == columns, inner, 0.0), axis=0, keepdims=True)
        r_row = lax.rsqrt(squares + NORM_EPS)
        r_col = row_scale(keys)
        b_col, b_row = 2.0 * jax.nn.sigmoid(raw_col), 2.0 * jax.nn.sigmoid(raw_row)
        lows.append(jnp.where(columns < rows, inner * (b_col * r_col) * r_row, 0.0))
        scales.append((r_col, r_row, b_col, b_row))
    blocks = []
    for low in lows:
        blocks += [low[:DIM, :DIM], low[DIM:, DIM:]]
    inverses = unit_lower_inverse(blocks)
    results = []
    for index, (queries, keys, values, raw_col, raw_row) in enumerate(heads):
        r_col, r_row, b_col, b_row = scales[index]
        upper, lower = inverses[2 * index], inverses[2 * index + 1]
        corner = mm3(split(lower), split(mm3(split(lows[index][DIM:, :DIM]), split(upper))))
        inverse = jnp.concatenate(
            [
                jnp.concatenate([upper, jnp.zeros_like(upper)], axis=1),
                jnp.concatenate([-corner, lower], axis=1),
            ],
            axis=0,
        )
        written = inverse * b_row
        erase = mm2(split(written * r_row), keys)
        insert = mm2(split(written), values)
        key_back = mm2(split(inverse * r_col), keys, 0, 0)
        scores = mm(queries, keys, 1, 1) * r_row
        frame, step = iota(scores.shape, 0), iota(scores.shape, 1)
        scores = jnp.where(step <= 2 * frame + 1, scores, 0.0)
        score_back = mm3(split(inverse), split(scores), 0, 1)
        eye = (iota((DIM, DIM), 0) == iota((DIM, DIM), 1)).astype(f32)
        erase_scaled = split(erase * r_col)
        transit = eye - (mm(keys, erase_scaled[0], 0, 0) + mm(keys, erase_scaled[1], 0, 0))
        back_scaled = split(key_back * b_col)
        offset = mm(values, back_scaled[0], 0, 0) + mm(values, back_scaled[1], 0, 0)
        weighted = score_back * b_col
        reads = queries.astype(f32) - mm2(split(weighted * r_col), keys, 0, 0)
        mixed = mm2(split(weighted), values, 0, 0)
        results.append((erase, insert, key_back, score_back, transit, offset, reads, mixed, r_row))
    return results


def kernel(
    q_ref, k_ref, v_ref, raw_ref, cot_ref, w_ref,
    proj_ref, gq_ref, gk_ref, gv_ref, gb_ref, gw_ref,
    bcol_ref, brow_ref,
    wg, wf, cotg, erase_s, insert_s, kback_s, sback_s, reads_s, mixed_s, rrow_s, gm_s, y_s,
    t_send, o_send, z_send, t_recv, o_recv, z_recv,
    s_send, d_send, s_recv, d_recv, mb_send, mb_full, mb_recv, gwp, gwh, gwr, gws, gwb,
    w_ss, w_rs, wx_ss, wx_rs, e_ss, e_rs, c_ss, c_rs, t_ss, t_rs, o_ss, o_rs, z_ss, z_rs,
    s_ss, s_rs, d_ss, d_rs, m_ss, m_rs, g_ss, g_rs, b_ss, b_rs,
):
    dp, me = lax.axis_index("dp"), lax.axis_index("seq")
    x, c = dp // 2, dp % 2
    y, z = me // SIDE, me % SIDE
    twin = x * 2 + (1 - c)

    def x_peer(step):
        return ((x + step) % SIDE) * 2 + c, me

    barrier = pltpu.get_barrier_semaphore()
    for step in range(1, SEQ):
        pl.semaphore_signal(barrier, inc=1, device_id=(dp, (me + step) % SEQ), device_id_type=MESH)
    for step in range(1, SIDE):
        pl.semaphore_signal(barrier, inc=1, device_id=x_peer(step), device_id_type=MESH)
    pl.semaphore_signal(barrier, inc=1, device_id=(twin, me), device_id_type=MESH)

    expand = (iota((STEPS, FRAMES), 0) // 2 == iota((STEPS, FRAMES), 1)).astype(bf16)
    raw_parts = thirds(raw_ref[...])
    columns = sum(mm(expand, part) for part in raw_parts)
    bcol_ref[...] = jnp.where(
        iota((STEPS, HEADS), 0) % 2 == 0, columns[:, :HEADS], columns[:, HEADS:]
    )
    rows = sum(mm(part, expand, 0, 1) for part in raw_parts)
    rows = jnp.where(iota((HEADS, STEPS), 1) % 2 == 0, rows[:HEADS], rows[HEADS:])
    for head in range(HEADS):
        brow_ref[head] = rows[head : head + 1]
    w_wide = w_ref[...].astype(f32)
    w_halves = jnp.concatenate([w_wide[:, : MODEL // 2], w_wide[:, MODEL // 2 :]], axis=0)
    wg[x, c, me] = w_halves.astype(bf16)
    cotg[x] = cot_ref[...]

    pl.semaphore_wait(barrier, SEQ - 1 + SIDE - 1 + 1)

    def remote(source, target, send_sem, recv_sem, device):
        return pltpu.make_async_remote_copy(
            src_ref=source, dst_ref=target, send_sem=send_sem, recv_sem=recv_sem,
            device_id=device, device_id_type=MESH,
        )

    def arrival(target, send_sem, recv_sem):
        remote(target, target, send_sem, recv_sem, (twin, me)).wait_recv()

    def w_copy(to):
        return remote(wg.at[x, c, me], wg.at[x, c, me], w_ss.at[to], w_rs.at[me], (dp, to))

    for step in range(1, SEQ):
        w_copy((me + step) % SEQ).start()

    before, after, across = (x + 3) % SIDE, (x + 1) % SIDE, (x + 2) % SIDE

    class Ring:
        def __init__(self, block, send_sems, recv_sems):
            self.block, self.send_sems, self.recv_sems = block, send_sems, recv_sems

        def copy(self, place, half, sem):
            ref = self.block(place, half)
            device = x_peer(1) if sem < 3 else x_peer(3)
            return remote(ref, ref, self.send_sems.at[sem], self.recv_sems.at[sem], device)

        def arrive(self, place, half, sem):
            arrival(self.block(place, half), self.send_sems.at[sem], self.recv_sems.at[sem])

        def start(self):
            for half in range(2):
                self.copy(x, half, half).start()
                self.copy(x, 1 - half, 3 + 1 - half).start()

        def relay(self):
            self.arrive(before, 0, 0)
            self.copy(before, 0, 2).start()
            self.arrive(after, 1, 4)
            self.copy(after, 1, 5).start()

        def near(self):
            self.arrive(before, 1, 1)
            self.arrive(after, 0, 3)

        def far(self):
            self.arrive(across, 0, 2)
            self.arrive(across, 1, 5)

        def sent(self):
            for half in range(2):
                self.copy(x, half, half).wait_send()
                self.copy(x, half, 3 + half).wait_send()
            self.copy(before, 0, 2).wait_send()
            self.copy(after, 1, 5).wait_send()

    w_ring = Ring(lambda place, half: wg.at[place, c, pl.ds(8 * half, 8)], wx_ss, wx_rs)
    cot_ring = Ring(lambda place, half: cotg.at[place, pl.ds(HALF * half, HALF)], c_ss, c_rs)
    places = (x, before, after, across)

    def core_copy(index):
        ref = wg.at[places[index], c]
        return remote(ref, ref, e_ss.at[index], e_rs.at[index], (twin, me))

    def head_lanes(head):
        return pl.ds(pl.multiple_of(head * DIM, DIM), DIM)

    def state_copies(head, half):
        owner = 2 * head + half
        rows = pl.ds(half * HALF, HALF)
        return (
            remote(t_send.at[head], t_recv.at[me], t_ss.at[owner], t_rs.at[me], (dp, owner)),
            remote(o_send.at[head, rows], o_recv.at[me], o_ss.at[owner], o_rs.at[me], (dp, owner)),
        )

    def adjoint_copy(head, half):
        owner = 2 * head + half
        rows = pl.ds(half * HALF, HALF)
        return remote(z_send.at[head, rows], z_recv.at[me], z_ss.at[owner], z_rs.at[me], (dp, owner))

    def forward_pair(index, carry):
        pair = (index + y) % SIDE
        heads = []
        for inner in range(2):
            head = 2 * pair + inner
            heads.append(
                (
                    q_ref[:, head_lanes(head)],
                    k_ref[:, head_lanes(head)],
                    v_ref[:, head_lanes(head)],
                    pick_column(bcol_ref[...], head),
                    brow_ref[head],
                )
            )
        for inner, result in enumerate(local_forward(heads)):
            head = 2 * pair + inner
            erase, insert, key_back, score_back, transit, offset, reads, mixed, r_row = result
            offset = offset.astype(bf16)
            t_send[head] = transit
            o_send[head] = offset
            for half in range(2):
                owner = 2 * head + half

                @pl.when(owner != me)
                def _():
                    for copy in state_copies(head, half):
                        copy.start()

                @pl.when(owner == me)
                def _():
                    t_recv[me] = transit
                    o_recv[me] = offset[half * HALF : (half + 1) * HALF]

            erase_s[0, head], erase_s[1, head] = split(erase)
            insert_s[head] = insert
            kback_s[0, head], kback_s[1, head] = split(key_back)
            sback_s[0, head], sback_s[1, head] = split(score_back)
            reads_s[head] = reads.astype(bf16)
            mixed_s[head] = mixed
            rrow_s[head] = r_row

        @pl.when(index == W_AT)
        def _():
            for step in range(1, SEQ):
                source = (me + step) % SEQ
                arrival(wg.at[x, c, source], w_ss.at[source], w_rs.at[source])
            w_ring.start()
            core_copy(0).start()

        @pl.when(index == RELAY_AT)
        def _():
            w_ring.relay()
            w_ring.near()
            core_copy(1).start()
            core_copy(2).start()

        return carry

    lax.fori_loop(0, HEADS // 2, forward_pair, 0)
    cot_ring.start()

    for step in range(1, SEQ):
        source = (me + step) % SEQ
        arrival(t_recv.at[source], t_ss.at[source], t_rs.at[source])
        arrival(o_recv.at[source], o_ss.at[source], o_rs.at[source])

    def send_state(buffer, target, value, segment, send_sems, recv_sems):
        buffer[segment] = value.astype(bf16)

        @pl.when(segment != me)
        def _():
            remote(
                buffer.at[segment], target.at[me], send_sems.at[segment], recv_sems.at[me], (dp, segment)
            ).start()

        @pl.when(segment == me)
        def _():
            target[me] = value.astype(bf16)

    def carry_state(segment, state):
        send_state(s_send, s_recv, state, segment, s_ss, s_rs)
        return mm3(split(state), split(t_recv[segment]), 1, 1) + o_recv[segment].astype(f32)

    last_state = lax.fori_loop(0, SEQ - 1, carry_state, jnp.zeros((HALF, DIM), f32))
    send_state(s_send, s_recv, last_state, SEQ - 1, s_ss, s_rs)

    w_ring.far()
    core_copy(3).start()

    def order_rows(place, core):
        def one(index, carry):
            first = wg[place, core, 2 * index].astype(f32)
            second = wg[place, core, 2 * index + 1].astype(f32)
            start = pl.multiple_of(((place * 2 + core) * 8 + index) * 16, 16)
            top = jnp.concatenate([first[:8], second[:8]], axis=0)
            bottom = jnp.concatenate([first[8:], second[8:]], axis=0)
            wf[pl.ds(start, 16), pl.ds(0, MODEL // 2)] = top.astype(bf16)
            wf[pl.ds(start, 16), pl.ds(MODEL // 2, MODEL // 2)] = bottom.astype(bf16)
            return carry

        lax.fori_loop(0, 8, one, 0, unroll=2)

    for place in places:
        order_rows(place, c)
    for index, place in enumerate(places):
        arrival(wg.at[place, 1 - c], e_ss.at[index], e_rs.at[index])
        order_rows(place, 1 - c)

    def gradient_pair(index, carry):
        pair = (index + y) % SIDE
        rows = wf[pl.ds(pl.multiple_of(pair * 2 * DIM, 2 * DIM), 2 * DIM), :]
        both = mm(cot_ref[...], rows, 1, 1).astype(bf16)
        for inner in range(2):
            head = 2 * pair + inner
            grad = both[:, inner * DIM : (inner + 1) * DIM]
            gm_s[head] = grad
            adjoint = mm(grad, reads_s[head], 0, 0).astype(bf16)
            z_send[head] = adjoint
            for half in range(2):
                owner = 2 * head + half

                @pl.when(owner != me)
                def _():
                    adjoint_copy(head, half).start()

                @pl.when(owner == me)
                def _():
                    z_recv[me] = adjoint[half * HALF : (half + 1) * HALF]

        return carry

    lax.fori_loop(0, HEADS // 2, gradient_pair, 0)
    cot_ring.relay()

    def early_gradient(head, carry):
        y_s[head] = mm2((sback_s[0, head], sback_s[1, head]), gm_s[head])
        return carry

    lax.fori_loop(0, HEADS, early_gradient, 0)

    for step in range(1, SEQ):
        source = (me + step) % SEQ
        arrival(s_recv.at[source], s_ss.at[source], s_rs.at[source])

    def head_state(buffer, head):
        return jnp.concatenate([buffer[2 * head], buffer[2 * head + 1]], axis=0)

    def mix_head(head, carry):
        mixed = (mm(reads_s[head], head_state(s_recv, head), 1, 1) + mixed_s[head]).astype(bf16)
        mb_send[head] = mixed
        mb_full[:, head_lanes(head)] = mixed
        return carry

    lax.fori_loop(0, HEADS, mix_head, 0)

    def mixed_copy(step):
        to = (x + step) % SIDE
        return remote(
            mb_send.at[pl.ds(2 * to, 2)], mb_recv.at[:, x], m_ss.at[step - 1], m_rs.at[step - 1], x_peer(step)
        )

    for step in range(1, SIDE):
        mixed_copy(step).start()
    mb_recv[0, x] = mb_send[2 * x]
    mb_recv[1, x] = mb_send[2 * x + 1]

    for step in range(1, SEQ):
        source = (me + step) % SEQ
        arrival(z_recv.at[source], z_ss.at[source], z_rs.at[source])

    def carry_adjoint(index, state):
        segment = SEQ - 1 - index
        send_state(d_send, d_recv, state, segment, d_ss, d_rs)
        return mm3(split(state), split(t_recv[segment])) + z_recv[segment].astype(f32)

    first_adjoint = lax.fori_loop(0, SEQ - 1, carry_adjoint, jnp.zeros((HALF, DIM), f32))
    send_state(d_send, d_recv, first_adjoint, 0, d_ss, d_rs)

    def project(index, carry):
        lanes = pl.ds(pl.multiple_of(index * COLS, COLS), COLS)
        proj_ref[:, lanes] = mm(mb_full[...], wf[:, lanes]).astype(bf16)
        return carry

    lax.fori_loop(0, MODEL // COLS, project, 0)

    cot_ring.near()
    cot_ring.far()
    for step in range(1, SIDE):
        source = (x - step + SIDE) % SIDE
        arrival(mb_recv.at[:, source], m_ss.at[step - 1], m_rs.at[step - 1])

    def weight_chunk(inner, chunk):
        mixed = mb_recv[inner].reshape(SIDE * FRAMES, DIM)
        lanes = pl.ds(chunk * COLS, COLS)
        return lanes, mm(mixed, cotg[:, :, lanes].reshape(SIDE * FRAMES, COLS), 0, 0)

    def weight_copy(chunk):
        lanes = pl.ds(chunk * COLS, COLS)
        return remote(
            gwh.at[:, lanes], gwr.at[:, lanes], g_ss.at[chunk], g_rs.at[chunk], (twin, me)
        )

    for chunk in range(MODEL // COLS):
        lanes, part = weight_chunk(1 - c, chunk)
        gwh[:, lanes] = part.astype(bf16)
        weight_copy(chunk).start()
    for chunk in range(MODEL // COLS):
        lanes, part = weight_chunk(c, chunk)
        gwp[:, lanes] = part

    for step in range(1, SEQ):
        source = (me + step) % SEQ
        arrival(d_recv.at[source], d_ss.at[source], d_rs.at[source])

    def block_copy(step):
        to = (me + step) % SEQ
        return remote(gws.at[to], gwb.at[me], b_ss.at[to], b_rs.at[me], (dp, to))

    def backward_head(head, raw_all):
        queries, keys = q_ref[:, head_lanes(head)], k_ref[:, head_lanes(head)]
        raw = pick_column(raw_all, head)
        b_col = 2.0 * jax.nn.sigmoid(raw)
        r_col, r_row = row_scale(keys), rrow_s[head]
        state, later = head_state(s_recv, head), head_state(d_recv, head)
        grad = gm_s[head]
        delta = insert_s[head] - mm2((erase_s[0, head], erase_s[1, head]), state, 1, 1)
        solved = y_s[head] + mm2((kback_s[0, head], kback_s[1, head]), later, 1, 1)
        scaled = b_col * solved
        gv_ref[:, head_lanes(head)] = scaled.astype(bf16)
        raw_grad = jnp.sum(solved * delta, axis=1, keepdims=True) * jax.nn.sigmoid(-raw)
        delta_parts, scaled_parts = split(delta), split(-scaled)
        score_grad = mm(grad, delta_parts[0], 1, 1) + mm(grad, delta_parts[1], 1, 1)
        frame, step = iota(score_grad.shape, 0), iota(score_grad.shape, 1)
        score_grad = jnp.where(step <= 2 * frame + 1, score_grad, 0.0)
        inner_grad = mm3(scaled_parts, delta_parts, 1, 1)
        row, column = iota(inner_grad.shape, 0), iota(inner_grad.shape, 1)
        inner_grad = jnp.where(column < row, inner_grad, 0.0)
        query_grad = mm(grad, state) + mm((score_grad * r_row).astype(bf16), keys)
        gq_ref[:, head_lanes(head)] = query_grad.astype(bf16)
        key_grad = mm(scaled_parts[0], state) + mm(delta_parts[0], later)
        key_grad = key_grad + mm(score_grad.astype(bf16), queries, 0, 0)
        key_grad = key_grad + mm((inner_grad * r_row).astype(bf16), keys)
        key_grad = key_grad + mm((inner_grad * r_col).astype(bf16), keys, 0, 0)
        unit = keys.astype(f32) * r_col
        along = jnp.sum(key_grad * unit, axis=1, keepdims=True)
        gk_ref[:, head_lanes(head)] = (r_col * (key_grad - unit * along)).astype(bf16)
        return raw_grad

    lane = iota((STEPS, HEADS), 1)

    def backward_pair(index, total):
        raw_all = bcol_ref[...]
        for inner in range(2):
            head = 2 * index + inner
            total = total + jnp.where(lane == head, backward_head(head, raw_all), 0.0)

        @pl.when(index == 0)
        def _():
            for chunk in range(MODEL // COLS):
                lanes = pl.ds(chunk * COLS, COLS)
                arrival(gwr.at[:, lanes], g_ss.at[chunk], g_rs.at[chunk])

            def one(index, carry):
                rows = pl.ds(pl.multiple_of(index * 16, 16), 16)
                block = gwp[rows] + gwr[rows].astype(f32)
                for inner in range(2):
                    part = block[8 * inner : 8 * inner + 8]
                    halves = [part[:, : MODEL // 2], part[:, MODEL // 2 :]]
                    gws[2 * index + inner] = jnp.concatenate(halves, axis=0).astype(bf16)
                return carry

            lax.fori_loop(0, SEQ // 2, one, 0)
            for step in range(1, SEQ):
                block_copy(step).start()
            gwb[me] = gws[me]

        return total

    raw_grad = lax.fori_loop(0, HEADS // 2, backward_pair, jnp.zeros((STEPS, HEADS), f32))
    raw_parts = thirds(raw_grad)
    for inner in range(2):
        chosen = 2 * iota((FRAMES, STEPS), 0) + inner == iota((FRAMES, STEPS), 1)
        chosen = chosen.astype(bf16)
        gb_ref[:, inner * HEADS : (inner + 1) * HEADS] = sum(mm(chosen, part) for part in raw_parts)

    for step in range(1, SEQ):
        source = (me + step) % SEQ
        arrival(gwb.at[source], b_ss.at[source], b_rs.at[source])
    total = gwb[0].astype(f32)
    for block in range(1, SEQ):
        total = total + gwb[block].astype(f32)
    gw_ref[:, : MODEL // 2] = total[:8]
    gw_ref[:, MODEL // 2 :] = total[8:]

    w_ring.sent()
    cot_ring.sent()
    for index in range(4):
        core_copy(index).wait_send()
        weight_copy(index).wait_send()
    for step in range(1, SIDE):
        mixed_copy(step).wait_send()
    for step in range(1, SEQ):
        other = (me + step) % SEQ
        block_copy(step).wait_send()
        w_copy(other).wait_send()
        remote(t_send.at[other // 2], t_recv.at[me], t_ss.at[other], t_rs.at[me], (dp, other)).wait_send()
        half_rows = pl.ds(pl.multiple_of((other % 2) * HALF, HALF), HALF)
        remote(
            o_send.at[other // 2, half_rows], o_recv.at[me], o_ss.at[other], o_rs.at[me], (dp, other)
        ).wait_send()
        remote(
            z_send.at[other // 2, half_rows], z_recv.at[me], z_ss.at[other], z_rs.at[me], (dp, other)
        ).wait_send()
        remote(s_send.at[other], s_recv.at[me], s_ss.at[other], s_rs.at[me], (dp, other)).wait_send()
        remote(d_send.at[other], d_recv.at[me], d_ss.at[other], d_rs.at[me], (dp, other)).wait_send()


def per_device(queries, key_vectors, values, beta_raw, cotangent, w_out):
    vmem = pl.BlockSpec(memory_space=pltpu.VMEM)
    dma = pltpu.SemaphoreType.DMA
    out = pl.pallas_call(
        kernel,
        out_shape=(
            jax.ShapeDtypeStruct((FRAMES, MODEL), bf16),
            jax.ShapeDtypeStruct((FRAMES, FEATURES), bf16),
            jax.ShapeDtypeStruct((STEPS, FEATURES), bf16),
            jax.ShapeDtypeStruct((STEPS, FEATURES), bf16),
            jax.ShapeDtypeStruct((FRAMES, 2 * HEADS), f32),
            jax.ShapeDtypeStruct((8, MODEL), f32),
        ),
        in_specs=[vmem] * 6,
        out_specs=[vmem] * 6,
        scratch_shapes=[
            pltpu.VMEM((STEPS, HEADS), f32),
            pltpu.VMEM((HEADS, 1, STEPS), f32),
            pltpu.VMEM((SIDE, 2, SEQ, 16, MODEL // 2), bf16),
            pltpu.VMEM((FEATURES, MODEL), bf16),
            pltpu.VMEM((SIDE, FRAMES, MODEL), bf16),
            pltpu.VMEM((2, HEADS, STEPS, DIM), bf16),
            pltpu.VMEM((HEADS, STEPS, DIM), f32),
            pltpu.VMEM((2, HEADS, STEPS, DIM), bf16),
            pltpu.VMEM((2, HEADS, STEPS, DIM), bf16),
            pltpu.VMEM((HEADS, FRAMES, DIM), bf16),
            pltpu.VMEM((HEADS, FRAMES, DIM), f32),
            pltpu.VMEM((HEADS, 1, STEPS), f32),
            pltpu.VMEM((HEADS, FRAMES, DIM), bf16),
            pltpu.VMEM((HEADS, STEPS, DIM), f32),
            pltpu.VMEM((HEADS, DIM, DIM), f32),
            pltpu.VMEM((HEADS, DIM, DIM), bf16),
            pltpu.VMEM((HEADS, DIM, DIM), bf16),
            pltpu.VMEM((SEQ, DIM, DIM), f32),
            pltpu.VMEM((SEQ, HALF, DIM), bf16),
            pltpu.VMEM((SEQ, HALF, DIM), bf16),
            pltpu.VMEM((SEQ, HALF, DIM), bf16),
            pltpu.VMEM((SEQ, HALF, DIM), bf16),
            pltpu.VMEM((SEQ, HALF, DIM), bf16),
            pltpu.VMEM((SEQ, HALF, DIM), bf16),
            pltpu.VMEM((HEADS, FRAMES, DIM), bf16),
            pltpu.VMEM((FRAMES, FEATURES), bf16),
            pltpu.VMEM((2, SIDE, FRAMES, DIM), bf16),
            pltpu.VMEM((DIM, MODEL), f32),
            pltpu.VMEM((DIM, MODEL), bf16),
            pltpu.VMEM((DIM, MODEL), bf16),
            pltpu.VMEM((SEQ, 16, MODEL // 2), bf16),
            pltpu.VMEM((SEQ, 16, MODEL // 2), bf16),
            dma((SEQ,)), dma((SEQ,)), dma((6,)), dma((6,)), dma((4,)), dma((4,)), dma((6,)), dma((6,)),
            dma((SEQ,)), dma((SEQ,)), dma((SEQ,)), dma((SEQ,)), dma((SEQ,)), dma((SEQ,)),
            dma((SEQ,)), dma((SEQ,)), dma((SEQ,)), dma((SEQ,)),
            dma((3,)), dma((3,)), dma((4,)), dma((4,)), dma((SEQ,)), dma((SEQ,)),
        ],
        compiler_params=pltpu.CompilerParams(
            collective_id=0, has_side_effects=True, vmem_limit_bytes=60 * 1024 * 1024
        ),
        name="delta_product",
    )(
        queries[0],
        key_vectors[0].reshape(STEPS, FEATURES),
        values[0].reshape(STEPS, FEATURES),
        beta_raw[0],
        cotangent[0],
        w_out,
    )
    projected, grad_query, grad_key, grad_value, grad_raw, grad_weight = out
    return (
        projected[None],
        grad_query[None],
        grad_key.reshape(1, FRAMES, 2, FEATURES),
        grad_value.reshape(1, FRAMES, 2, FEATURES),
        grad_raw[None],
        grad_weight,
    )


def solution(mesh):
    in_specs = (
        P("dp", "seq", None),
        P("dp", "seq", None, None),
        P("dp", "seq", None, None),
        P("dp", "seq", None),
        P("dp", "seq", None),
        P(("dp", "seq"), None),
    )
    out_specs = (
        P("dp", "seq", None),
        P("dp", "seq", None),
        P("dp", "seq", None, None),
        P("dp", "seq", None, None),
        P("dp", "seq", None),
        P(("dp", "seq"), None),
    )
    return jax.shard_map(
        per_device, mesh=mesh, in_specs=in_specs, out_specs=out_specs, check_vma=False
    )
```

```python
import jax
import jax.numpy as jnp
from jax import lax
from jax.experimental import pallas as pl
from jax.experimental.pallas import tpu as pltpu
from jax.sharding import PartitionSpec as P

f32, bf16 = jnp.float32, jnp.bfloat16
MESH = pl.DeviceIdType.MESH
NORM_EPS = 1e-06
HEADS = 8
DIM = 128
HALF = 64
FRAMES = 128
STEPS = 256
MODEL = 2048
FEATURES = HEADS * DIM
SEQ = 16
SIDE = 4
COLS = 512
W_AT = 1
RELAY_AT = 5
WEIGHT_AT = 0
BLOCK_AT = 1


def mm(a, b, ca=1, cb=0):
    return lax.dot_general(a, b, (((ca,), (cb,)), ((), ())), preferred_element_type=f32)


def split(x):
    high = x.astype(bf16)
    return high, (x - high.astype(f32)).astype(bf16)


def mm2(a, b, ca=1, cb=0):
    return mm(a[0], b, ca, cb) + mm(a[1], b, ca, cb)


def mm3(a, b, ca=1, cb=0):
    return mm(a[0], b[0], ca, cb) + (mm(a[0], b[1], ca, cb) + mm(a[1], b[0], ca, cb))


def thirds(x):
    high = x.astype(bf16)
    rest = x - high.astype(f32)
    middle = rest.astype(bf16)
    return high, middle, (rest - middle.astype(f32)).astype(bf16)


def iota(shape, axis):
    return lax.broadcasted_iota(jnp.int32, shape, axis)


def unit_lower_inverse(blocks):
    shape = blocks[0].shape
    rows, columns = iota(shape, 0), iota(shape, 1)
    differing = rows ^ columns
    eye = (rows == columns).astype(f32)
    inverses = [eye - jnp.where(differing == 1, low, 0.0) for low in blocks]
    size = 2
    while size < shape[0]:
        mask = (differing >= size) & (differing < 2 * size)
        parts = [split(inverse) for inverse in inverses]
        offs = [split(jnp.where(mask, low, 0.0)) for low in blocks]
        firsts = [split(mm3(part, off)) for part, off in zip(parts, offs)]
        inverses = [inv - mm3(first, part) for inv, first, part in zip(inverses, firsts, parts)]
        size *= 2
    return inverses


def pick_column(array, head):
    return jnp.sum(jnp.where(iota(array.shape, 1) == head, array, 0.0), axis=1, keepdims=True)


def row_scale(keys):
    wide = keys.astype(f32)
    return lax.rsqrt(jnp.sum(wide * wide, axis=1, keepdims=True) + NORM_EPS)


def local_transits(heads):
    lows, scales = [], []
    for keys, values, raw_col, raw_row in heads:
        inner = mm(keys, keys, 1, 1)
        rows, columns = iota(inner.shape, 0), iota(inner.shape, 1)
        squares = jnp.sum(jnp.where(rows == columns, inner, 0.0), axis=0, keepdims=True)
        r_row = lax.rsqrt(squares + NORM_EPS)
        r_col = row_scale(keys)
        b_col, b_row = 2.0 * jax.nn.sigmoid(raw_col), 2.0 * jax.nn.sigmoid(raw_row)
        lows.append(jnp.where(columns < rows, inner * (b_col * r_col) * r_row, 0.0))
        scales.append((r_col, r_row, b_col, b_row))
    blocks = []
    for low in lows:
        blocks += [low[:DIM, :DIM], low[DIM:, DIM:]]
    inverses = unit_lower_inverse(blocks)
    results = []
    for index, (keys, values, raw_col, raw_row) in enumerate(heads):
        r_col, r_row, b_col, b_row = scales[index]
        upper, lower = inverses[2 * index], inverses[2 * index + 1]
        corner = mm3(split(lower), split(mm3(split(lows[index][DIM:, :DIM]), split(upper))))
        inverse = jnp.concatenate(
            [
                jnp.concatenate([upper, jnp.zeros_like(upper)], axis=1),
                jnp.concatenate([-corner, lower], axis=1),
            ],
            axis=0,
        )
        erase = mm2(split(inverse * (b_row * r_row)), keys)
        key_back = mm2(split(inverse * r_col), keys, 0, 0)
        eye = (iota((DIM, DIM), 0) == iota((DIM, DIM), 1)).astype(f32)
        erase_scaled = split(erase * r_col)
        transit = eye - (mm(keys, erase_scaled[0], 0, 0) + mm(keys, erase_scaled[1], 0, 0))
        back_scaled = split(key_back * b_col)
        offset = mm(values, back_scaled[0], 0, 0) + mm(values, back_scaled[1], 0, 0)
        results.append((inverse, erase, key_back, transit, offset, r_row))
    return results


def local_reads(queries, keys, values, raw_col, raw_row, inverse_parts, r_row):
    r_col = row_scale(keys)
    b_col, b_row = 2.0 * jax.nn.sigmoid(raw_col), 2.0 * jax.nn.sigmoid(raw_row)
    inverse = inverse_parts[0].astype(f32) + inverse_parts[1].astype(f32)
    insert = mm2(split(inverse * b_row), values)
    scores = mm(queries, keys, 1, 1) * r_row
    frame, step = iota(scores.shape, 0), iota(scores.shape, 1)
    scores = jnp.where(step <= 2 * frame + 1, scores, 0.0)
    score_back = mm3(inverse_parts, split(scores), 0, 1)
    weighted = score_back * b_col
    reads = queries.astype(f32) - mm2(split(weighted * r_col), keys, 0, 0)
    mixed = mm2(split(weighted), values, 0, 0)
    return insert, score_back, reads, mixed


def kernel(
    q_ref, k_ref, v_ref, raw_ref, cot_ref, w_ref,
    proj_ref, gq_ref, gk_ref, gv_ref, gb_ref, gw_ref,
    bcol_ref, brow_ref, k_s, v_s, inv_s,
    wg, wf, cotg, erase_s, insert_s, kback_s, sback_s, reads_s, mixed_s, rrow_s, gm_s, y_s,
    t_send, o_send, z_send, t_recv, o_recv, z_recv,
    s_send, d_send, s_recv, d_recv, mb_send, mb_full, mb_recv, gwp, gwh, gwr, gws, gwb,
    w_ss, w_rs, wx_ss, wx_rs, e_ss, e_rs, c_ss, c_rs, t_ss, t_rs, o_ss, o_rs, z_ss, z_rs,
    s_ss, s_rs, d_ss, d_rs, m_ss, m_rs, g_ss, g_rs, b_ss, b_rs,
):
    dp, me = lax.axis_index("dp"), lax.axis_index("seq")
    x, c = dp // 2, dp % 2
    y, z = me // SIDE, me % SIDE
    twin = x * 2 + (1 - c)

    def x_peer(step):
        return ((x + step) % SIDE) * 2 + c, me

    barrier = pltpu.get_barrier_semaphore()
    for step in range(1, SEQ):
        pl.semaphore_signal(barrier, inc=1, device_id=(dp, (me + step) % SEQ), device_id_type=MESH)
    for step in range(1, SIDE):
        pl.semaphore_signal(barrier, inc=1, device_id=x_peer(step), device_id_type=MESH)
    pl.semaphore_signal(barrier, inc=1, device_id=(twin, me), device_id_type=MESH)

    expand = (iota((STEPS, FRAMES), 0) // 2 == iota((STEPS, FRAMES), 1)).astype(bf16)
    raw_parts = thirds(raw_ref[...])
    columns = sum(mm(expand, part, 1, 1) for part in raw_parts)
    bcol_ref[...] = jnp.where(
        iota((STEPS, HEADS), 0) % 2 == 0, columns[:, :HEADS], columns[:, HEADS:]
    )
    rows = sum(mm(part, expand, 1, 1) for part in raw_parts)
    rows = jnp.where(iota((HEADS, STEPS), 1) % 2 == 0, rows[:HEADS], rows[HEADS:])
    for head in range(HEADS):
        brow_ref[head] = rows[head : head + 1]
    w_wide = w_ref[...].astype(f32)
    w_halves = jnp.concatenate([w_wide[:, : MODEL // 2], w_wide[:, MODEL // 2 :]], axis=0)
    wg[x, c, me] = w_halves.astype(bf16)
    cotg[x] = cot_ref[...]

    pl.semaphore_wait(barrier, SEQ - 1 + SIDE - 1 + 1)

    def remote(source, target, send_sem, recv_sem, device):
        return pltpu.make_async_remote_copy(
            src_ref=source, dst_ref=target, send_sem=send_sem, recv_sem=recv_sem,
            device_id=device, device_id_type=MESH,
        )

    def arrival(target, send_sem, recv_sem):
        remote(target, target, send_sem, recv_sem, (twin, me)).wait_recv()

    def w_copy(to):
        return remote(wg.at[x, c, me], wg.at[x, c, me], w_ss.at[to], w_rs.at[me], (dp, to))

    for step in range(1, SEQ):
        w_copy((me + step) % SEQ).start()

    before, after, across = (x + 3) % SIDE, (x + 1) % SIDE, (x + 2) % SIDE

    class Ring:
        def __init__(self, block, send_sems, recv_sems):
            self.block, self.send_sems, self.recv_sems = block, send_sems, recv_sems

        def copy(self, place, half, sem):
            ref = self.block(place, half)
            device = x_peer(1) if sem < 3 else x_peer(3)
            return remote(ref, ref, self.send_sems.at[sem], self.recv_sems.at[sem], device)

        def arrive(self, place, half, sem):
            arrival(self.block(place, half), self.send_sems.at[sem], self.recv_sems.at[sem])

        def start(self):
            for half in range(2):
                self.copy(x, half, half).start()
                self.copy(x, 1 - half, 3 + 1 - half).start()

        def relay(self):
            self.arrive(before, 0, 0)
            self.copy(before, 0, 2).start()
            self.arrive(after, 1, 4)
            self.copy(after, 1, 5).start()

        def near(self):
            self.arrive(before, 1, 1)
            self.arrive(after, 0, 3)

        def far(self):
            self.arrive(across, 0, 2)
            self.arrive(across, 1, 5)

        def sent(self):
            for half in range(2):
                self.copy(x, half, half).wait_send()
                self.copy(x, half, 3 + half).wait_send()
            self.copy(before, 0, 2).wait_send()
            self.copy(after, 1, 5).wait_send()

    w_ring = Ring(lambda place, half: wg.at[place, c, pl.ds(8 * half, 8)], wx_ss, wx_rs)
    cot_ring = Ring(lambda place, half: cotg.at[place, pl.ds(HALF * half, HALF)], c_ss, c_rs)
    places = (x, before, after, across)

    def core_copy(index):
        ref = wg.at[places[index], c]
        return remote(ref, ref, e_ss.at[index], e_rs.at[index], (twin, me))

    def head_lanes(head):
        return pl.ds(pl.multiple_of(head * DIM, DIM), DIM)

    def state_copies(head, half):
        owner = 2 * head + half
        rows = pl.ds(half * HALF, HALF)
        return (
            remote(t_send.at[head], t_recv.at[me], t_ss.at[owner], t_rs.at[me], (dp, owner)),
            remote(o_send.at[head, rows], o_recv.at[me], o_ss.at[owner], o_rs.at[me], (dp, owner)),
        )

    def adjoint_copy(head, half):
        owner = 2 * head + half
        rows = pl.ds(half * HALF, HALF)
        return remote(z_send.at[head, rows], z_recv.at[me], z_ss.at[owner], z_rs.at[me], (dp, owner))

    def transit_pair(index, carry):
        pair = (index + y) % SIDE
        heads = []
        for inner in range(2):
            head = 2 * pair + inner
            keys = k_ref[:, :, head_lanes(head)].reshape(STEPS, DIM)
            values = v_ref[:, :, head_lanes(head)].reshape(STEPS, DIM)
            k_s[head], v_s[head] = keys, values
            heads.append((keys, values, pick_column(bcol_ref[...], head), brow_ref[head]))
        for inner, result in enumerate(local_transits(heads)):
            head = 2 * pair + inner
            inverse, erase, key_back, transit, offset, r_row = result
            offset = offset.astype(bf16)
            t_send[head] = transit
            o_send[head] = offset
            for half in range(2):
                owner = 2 * head + half

                @pl.when(owner != me)
                def _():
                    for copy in state_copies(head, half):
                        copy.start()

                @pl.when(owner == me)
                def _():
                    t_recv[me] = transit
                    o_recv[me] = offset[half * HALF : (half + 1) * HALF]

            inv_s[0, head], inv_s[1, head] = split(inverse)
            erase_s[0, head], erase_s[1, head] = split(erase)
            kback_s[0, head], kback_s[1, head] = split(key_back)
            rrow_s[head] = r_row
        advance(index)
        return carry

    def reads_pair(index, carry):
        for inner in range(2):
            head = 2 * index + inner
            insert, score_back, reads, mixed = local_reads(
                q_ref[:, head_lanes(head)], k_s[head], v_s[head],
                pick_column(bcol_ref[...], head), brow_ref[head],
                (inv_s[0, head], inv_s[1, head]), rrow_s[head],
            )
            insert_s[head] = insert
            sback_s[0, head], sback_s[1, head] = split(score_back)
            reads_s[head] = reads.astype(bf16)
            mixed_s[head] = mixed
        advance(index + HEADS // 2)
        return carry

    def advance(index):
        @pl.when(index == W_AT)
        def _():
            for step in range(1, SEQ):
                source = (me + step) % SEQ
                arrival(wg.at[x, c, source], w_ss.at[source], w_rs.at[source])
            w_ring.start()
            core_copy(0).start()

        @pl.when(index == RELAY_AT)
        def _():
            w_ring.relay()
            w_ring.near()
            core_copy(1).start()
            core_copy(2).start()

    lax.fori_loop(0, HEADS // 2, transit_pair, 0)
    lax.fori_loop(0, HEADS // 2, reads_pair, 0)
    w_ring.far()
    core_copy(3).start()
    cot_ring.start()

    def order_rows(place, core):
        def one(index, carry):
            first = wg[place, core, 2 * index].astype(f32)
            second = wg[place, core, 2 * index + 1].astype(f32)
            start = pl.multiple_of(((place * 2 + core) * 8 + index) * 16, 16)
            top = jnp.concatenate([first[:8], second[:8]], axis=0)
            bottom = jnp.concatenate([first[8:], second[8:]], axis=0)
            wf[pl.ds(start, 16), pl.ds(0, MODEL // 2)] = top.astype(bf16)
            wf[pl.ds(start, 16), pl.ds(MODEL // 2, MODEL // 2)] = bottom.astype(bf16)
            return carry

        lax.fori_loop(0, 8, one, 0, unroll=2)

    for place in places:
        order_rows(place, c)
    for index, place in enumerate(places):
        arrival(wg.at[place, 1 - c], e_ss.at[index], e_rs.at[index])
        order_rows(place, 1 - c)

    def gradient_pair(index, carry):
        pair = (index + y) % SIDE
        rows = wf[pl.ds(pl.multiple_of(pair * 2 * DIM, 2 * DIM), 2 * DIM), :]
        both = mm(cot_ref[...], rows, 1, 1).astype(bf16)
        for inner in range(2):
            head = 2 * pair + inner
            grad = both[:, inner * DIM : (inner + 1) * DIM]
            gm_s[head] = grad
            adjoint = mm(grad, reads_s[head], 0, 0).astype(bf16)
            z_send[head] = adjoint
            for half in range(2):
                owner = 2 * head + half

                @pl.when(owner != me)
                def _():
                    adjoint_copy(head, half).start()

                @pl.when(owner == me)
                def _():
                    z_recv[me] = adjoint[half * HALF : (half + 1) * HALF]

        return carry

    lax.fori_loop(0, HEADS // 2, gradient_pair, 0)

    def early_gradient(head, carry):
        y_s[head] = mm2((sback_s[0, head], sback_s[1, head]), gm_s[head])
        return carry

    lax.fori_loop(0, HEADS, early_gradient, 0)

    for step in range(1, SEQ):
        source = (me + step) % SEQ
        arrival(t_recv.at[source], t_ss.at[source], t_rs.at[source])
        arrival(o_recv.at[source], o_ss.at[source], o_rs.at[source])
        arrival(z_recv.at[source], z_ss.at[source], z_rs.at[source])

    def send_state(buffer, target, value, segment, send_sems, recv_sems):
        buffer[segment] = value.astype(bf16)

        @pl.when(segment != me)
        def _():
            remote(
                buffer.at[segment], target.at[me], send_sems.at[segment], recv_sems.at[me], (dp, segment)
            ).start()

        @pl.when(segment == me)
        def _():
            target[me] = value.astype(bf16)

    def carry_both(index, carry):
        state, adjoint = carry
        last = SEQ - 1 - index
        send_state(s_send, s_recv, state, index, s_ss, s_rs)
        send_state(d_send, d_recv, adjoint, last, d_ss, d_rs)
        state = mm3(split(state), split(t_recv[index]), 1, 1) + o_recv[index].astype(f32)
        adjoint = mm3(split(adjoint), split(t_recv[last])) + z_recv[last].astype(f32)
        return state, adjoint

    empty = jnp.zeros((HALF, DIM), f32)
    state, adjoint = lax.fori_loop(0, SEQ - 1, carry_both, (empty, empty))
    send_state(s_send, s_recv, state, SEQ - 1, s_ss, s_rs)
    send_state(d_send, d_recv, adjoint, 0, d_ss, d_rs)
    cot_ring.relay()

    for step in range(1, SEQ):
        source = (me + step) % SEQ
        arrival(s_recv.at[source], s_ss.at[source], s_rs.at[source])

    def head_state(buffer, head):
        return jnp.concatenate([buffer[2 * head], buffer[2 * head + 1]], axis=0)

    def mix_head(head, carry):
        mixed = (mm(reads_s[head], head_state(s_recv, head), 1, 1) + mixed_s[head]).astype(bf16)
        mb_send[head] = mixed
        mb_full[:, head_lanes(head)] = mixed
        return carry

    lax.fori_loop(0, HEADS, mix_head, 0)

    def mixed_copy(step):
        to = (x + step) % SIDE
        return remote(
            mb_send.at[pl.ds(2 * to, 2)], mb_recv.at[:, x], m_ss.at[step - 1], m_rs.at[step - 1], x_peer(step)
        )

    for step in range(1, SIDE):
        mixed_copy(step).start()
    mb_recv[0, x] = mb_send[2 * x]
    mb_recv[1, x] = mb_send[2 * x + 1]

    def project(index, carry):
        lanes = pl.ds(pl.multiple_of(index * COLS, COLS), COLS)
        proj_ref[:, lanes] = mm(mb_full[...], wf[:, lanes]).astype(bf16)
        return carry

    lax.fori_loop(0, MODEL // COLS, project, 0)

    def weight_chunk(inner, chunk):
        mixed = mb_recv[inner].reshape(SIDE * FRAMES, DIM)
        lanes = pl.ds(chunk * COLS, COLS)
        return lanes, mm(mixed, cotg[:, :, lanes].reshape(SIDE * FRAMES, COLS), 0, 0)

    def weight_copy(chunk):
        lanes = pl.ds(chunk * COLS, COLS)
        return remote(
            gwh.at[:, lanes], gwr.at[:, lanes], g_ss.at[chunk], g_rs.at[chunk], (twin, me)
        )

    def weight_parts():
        cot_ring.near()
        cot_ring.far()
        for step in range(1, SIDE):
            source = (x - step + SIDE) % SIDE
            arrival(mb_recv.at[:, source], m_ss.at[step - 1], m_rs.at[step - 1])
        for chunk in range(MODEL // COLS):
            lanes, part = weight_chunk(1 - c, chunk)
            gwh[:, lanes] = part.astype(bf16)
            weight_copy(chunk).start()
        for chunk in range(MODEL // COLS):
            lanes, part = weight_chunk(c, chunk)
            gwp[:, lanes] = part

    if WEIGHT_AT < 0:
        weight_parts()

    for step in range(1, SEQ):
        source = (me + step) % SEQ
        arrival(d_recv.at[source], d_ss.at[source], d_rs.at[source])

    def block_copy(step):
        to = (me + step) % SEQ
        return remote(gws.at[to], gwb.at[me], b_ss.at[to], b_rs.at[me], (dp, to))

    def backward_head(head, raw_all):
        queries, keys = q_ref[:, head_lanes(head)], k_s[head]
        raw = pick_column(raw_all, head)
        b_col = 2.0 * jax.nn.sigmoid(raw)
        r_col, r_row = row_scale(keys), rrow_s[head]
        state, later = head_state(s_recv, head), head_state(d_recv, head)
        grad = gm_s[head]
        delta = insert_s[head] - mm2((erase_s[0, head], erase_s[1, head]), state, 1, 1)
        solved = y_s[head] + mm2((kback_s[0, head], kback_s[1, head]), later, 1, 1)
        scaled = b_col * solved
        gv_ref[:, :, head_lanes(head)] = scaled.astype(bf16).reshape(FRAMES, 2, DIM)
        raw_grad = jnp.sum(solved * delta, axis=1, keepdims=True) * jax.nn.sigmoid(-raw)
        delta_parts, scaled_parts = split(delta), split(-scaled)
        score_grad = mm(grad, delta_parts[0], 1, 1) + mm(grad, delta_parts[1], 1, 1)
        frame, step = iota(score_grad.shape, 0), iota(score_grad.shape, 1)
        score_grad = jnp.where(step <= 2 * frame + 1, score_grad, 0.0)
        inner_grad = mm3(scaled_parts, delta_parts, 1, 1)
        row, column = iota(inner_grad.shape, 0), iota(inner_grad.shape, 1)
        inner_grad = jnp.where(column < row, inner_grad, 0.0)
        query_grad = mm(grad, state) + mm((score_grad * r_row).astype(bf16), keys)
        gq_ref[:, head_lanes(head)] = query_grad.astype(bf16)
        key_grad = mm(scaled_parts[0], state) + mm(delta_parts[0], later)
        key_grad = key_grad + mm(score_grad.astype(bf16), queries, 0, 0)
        key_grad = key_grad + mm((inner_grad * r_row).astype(bf16), keys)
        key_grad = key_grad + mm((inner_grad * r_col).astype(bf16), keys, 0, 0)
        unit = keys.astype(f32) * r_col
        along = jnp.sum(key_grad * unit, axis=1, keepdims=True)
        key_grad = (r_col * (key_grad - unit * along)).astype(bf16)
        gk_ref[:, :, head_lanes(head)] = key_grad.reshape(FRAMES, 2, DIM)
        return raw_grad

    lane = iota((STEPS, HEADS), 1)

    def backward_pair(index, total):
        raw_all = bcol_ref[...]
        for inner in range(2):
            head = 2 * index + inner
            total = total + jnp.where(lane == head, backward_head(head, raw_all), 0.0)

        @pl.when(index == WEIGHT_AT)
        def _():
            weight_parts()

        @pl.when(index == BLOCK_AT)
        def _():
            for chunk in range(MODEL // COLS):
                lanes = pl.ds(chunk * COLS, COLS)
                arrival(gwr.at[:, lanes], g_ss.at[chunk], g_rs.at[chunk])

            def one(index, carry):
                rows = pl.ds(pl.multiple_of(index * 16, 16), 16)
                block = gwp[rows] + gwr[rows].astype(f32)
                for inner in range(2):
                    part = block[8 * inner : 8 * inner + 8]
                    halves = [part[:, : MODEL // 2], part[:, MODEL // 2 :]]
                    gws[2 * index + inner] = jnp.concatenate(halves, axis=0).astype(bf16)
                return carry

            lax.fori_loop(0, SEQ // 2, one, 0)
            for step in range(1, SEQ):
                block_copy(step).start()
            gwb[me] = gws[me]

        return total

    raw_grad = lax.fori_loop(0, HEADS // 2, backward_pair, jnp.zeros((STEPS, HEADS), f32))
    raw_parts = thirds(raw_grad)
    for inner in range(2):
        chosen = 2 * iota((FRAMES, STEPS), 0) + inner == iota((FRAMES, STEPS), 1)
        chosen = chosen.astype(bf16)
        gb_ref[inner * HEADS : (inner + 1) * HEADS] = sum(mm(part, chosen, 0, 1) for part in raw_parts)

    for step in range(1, SEQ):
        source = (me + step) % SEQ
        arrival(gwb.at[source], b_ss.at[source], b_rs.at[source])
    total = gwb[0].astype(f32)
    for block in range(1, SEQ):
        total = total + gwb[block].astype(f32)
    gw_ref[:, : MODEL // 2] = total[:8]
    gw_ref[:, MODEL // 2 :] = total[8:]

    w_ring.sent()
    cot_ring.sent()
    for index in range(4):
        core_copy(index).wait_send()
        weight_copy(index).wait_send()
    for step in range(1, SIDE):
        mixed_copy(step).wait_send()
    for step in range(1, SEQ):
        other = (me + step) % SEQ
        block_copy(step).wait_send()
        w_copy(other).wait_send()
        remote(t_send.at[other // 2], t_recv.at[me], t_ss.at[other], t_rs.at[me], (dp, other)).wait_send()
        half_rows = pl.ds(pl.multiple_of((other % 2) * HALF, HALF), HALF)
        remote(
            o_send.at[other // 2, half_rows], o_recv.at[me], o_ss.at[other], o_rs.at[me], (dp, other)
        ).wait_send()
        remote(
            z_send.at[other // 2, half_rows], z_recv.at[me], z_ss.at[other], z_rs.at[me], (dp, other)
        ).wait_send()
        remote(s_send.at[other], s_recv.at[me], s_ss.at[other], s_rs.at[me], (dp, other)).wait_send()
        remote(d_send.at[other], d_recv.at[me], d_ss.at[other], d_rs.at[me], (dp, other)).wait_send()


def per_device(queries, key_vectors, values, beta_raw, cotangent, w_out):
    vmem = pl.BlockSpec(memory_space=pltpu.VMEM)
    dma = pltpu.SemaphoreType.DMA
    out = pl.pallas_call(
        kernel,
        out_shape=(
            jax.ShapeDtypeStruct((FRAMES, MODEL), bf16),
            jax.ShapeDtypeStruct((FRAMES, FEATURES), bf16),
            jax.ShapeDtypeStruct((FRAMES, 2, FEATURES), bf16),
            jax.ShapeDtypeStruct((FRAMES, 2, FEATURES), bf16),
            jax.ShapeDtypeStruct((2 * HEADS, FRAMES), f32),
            jax.ShapeDtypeStruct((8, MODEL), f32),
        ),
        in_specs=[vmem] * 6,
        out_specs=[vmem] * 6,
        scratch_shapes=[
            pltpu.VMEM((STEPS, HEADS), f32),
            pltpu.VMEM((HEADS, 1, STEPS), f32),
            pltpu.VMEM((HEADS, STEPS, DIM), bf16),
            pltpu.VMEM((HEADS, STEPS, DIM), bf16),
            pltpu.VMEM((2, HEADS, STEPS, STEPS), bf16),
            pltpu.VMEM((SIDE, 2, SEQ, 16, MODEL // 2), bf16),
            pltpu.VMEM((FEATURES, MODEL), bf16),
            pltpu.VMEM((SIDE, FRAMES, MODEL), bf16),
            pltpu.VMEM((2, HEADS, STEPS, DIM), bf16),
            pltpu.VMEM((HEADS, STEPS, DIM), f32),
            pltpu.VMEM((2, HEADS, STEPS, DIM), bf16),
            pltpu.VMEM((2, HEADS, STEPS, DIM), bf16),
            pltpu.VMEM((HEADS, FRAMES, DIM), bf16),
            pltpu.VMEM((HEADS, FRAMES, DIM), f32),
            pltpu.VMEM((HEADS, 1, STEPS), f32),
            pltpu.VMEM((HEADS, FRAMES, DIM), bf16),
            pltpu.VMEM((HEADS, STEPS, DIM), f32),
            pltpu.VMEM((HEADS, DIM, DIM), f32),
            pltpu.VMEM((HEADS, DIM, DIM), bf16),
            pltpu.VMEM((HEADS, DIM, DIM), bf16),
            pltpu.VMEM((SEQ, DIM, DIM), f32),
            pltpu.VMEM((SEQ, HALF, DIM), bf16),
            pltpu.VMEM((SEQ, HALF, DIM), bf16),
            pltpu.VMEM((SEQ, HALF, DIM), bf16),
            pltpu.VMEM((SEQ, HALF, DIM), bf16),
            pltpu.VMEM((SEQ, HALF, DIM), bf16),
            pltpu.VMEM((SEQ, HALF, DIM), bf16),
            pltpu.VMEM((HEADS, FRAMES, DIM), bf16),
            pltpu.VMEM((FRAMES, FEATURES), bf16),
            pltpu.VMEM((2, SIDE, FRAMES, DIM), bf16),
            pltpu.VMEM((DIM, MODEL), f32),
            pltpu.VMEM((DIM, MODEL), bf16),
            pltpu.VMEM((DIM, MODEL), bf16),
            pltpu.VMEM((SEQ, 16, MODEL // 2), bf16),
            pltpu.VMEM((SEQ, 16, MODEL // 2), bf16),
            dma((SEQ,)), dma((SEQ,)), dma((6,)), dma((6,)), dma((4,)), dma((4,)), dma((6,)), dma((6,)),
            dma((SEQ,)), dma((SEQ,)), dma((SEQ,)), dma((SEQ,)), dma((SEQ,)), dma((SEQ,)),
            dma((SEQ,)), dma((SEQ,)), dma((SEQ,)), dma((SEQ,)),
            dma((3,)), dma((3,)), dma((4,)), dma((4,)), dma((SEQ,)), dma((SEQ,)),
        ],
        compiler_params=pltpu.CompilerParams(
            collective_id=0, has_side_effects=True, vmem_limit_bytes=60 * 1024 * 1024
        ),
        name="delta_product",
    )(
        queries[0],
        key_vectors[0],
        values[0],
        beta_raw[0].T,
        cotangent[0],
        w_out,
    )
    projected, grad_query, grad_key, grad_value, grad_raw, grad_weight = out
    return (
        projected[None],
        grad_query[None],
        grad_key[None],
        grad_value[None],
        grad_raw.T[None],
        grad_weight,
    )


def solution(mesh):
    in_specs = (
        P("dp", "seq", None),
        P("dp", "seq", None, None),
        P("dp", "seq", None, None),
        P("dp", "seq", None),
        P("dp", "seq", None),
        P(("dp", "seq"), None),
    )
    out_specs = (
        P("dp", "seq", None),
        P("dp", "seq", None),
        P("dp", "seq", None, None),
        P("dp", "seq", None, None),
        P("dp", "seq", None),
        P(("dp", "seq"), None),
    )
    return jax.shard_map(
        per_device, mesh=mesh, in_specs=in_specs, out_specs=out_specs, check_vma=False
    )
```

```python
import jax
import jax.numpy as jnp
from jax import lax
from jax.experimental import pallas as pl
from jax.experimental.pallas import tpu as pltpu
from jax.sharding import PartitionSpec as P

f32, bf16 = jnp.float32, jnp.bfloat16
MESH = pl.DeviceIdType.MESH
NORM_EPS = 1e-06
HEADS = 8
DIM = 128
HALF = 64
FRAMES = 128
STEPS = 256
MODEL = 2048
FEATURES = HEADS * DIM
SEQ = 16
SIDE = 4
COLS = 512
W_AT = 1
RELAY_AT = 5
WEIGHT_AT = -1
BLOCK_AT = 0
FAR_FIRST = 1
RELAY_SPOT = 0


def mm(a, b, ca=1, cb=0):
    return lax.dot_general(a, b, (((ca,), (cb,)), ((), ())), preferred_element_type=f32)


def split(x):
    high = x.astype(bf16)
    return high, (x - high.astype(f32)).astype(bf16)


def mm2(a, b, ca=1, cb=0):
    return mm(a[0], b, ca, cb) + mm(a[1], b, ca, cb)


def mm3(a, b, ca=1, cb=0):
    return mm(a[0], b[0], ca, cb) + (mm(a[0], b[1], ca, cb) + mm(a[1], b[0], ca, cb))


def thirds(x):
    high = x.astype(bf16)
    rest = x - high.astype(f32)
    middle = rest.astype(bf16)
    return high, middle, (rest - middle.astype(f32)).astype(bf16)


def iota(shape, axis):
    return lax.broadcasted_iota(jnp.int32, shape, axis)


def unit_lower_inverse(blocks):
    shape = blocks[0].shape
    rows, columns = iota(shape, 0), iota(shape, 1)
    differing = rows ^ columns
    eye = (rows == columns).astype(f32)
    inverses = [eye - jnp.where(differing == 1, low, 0.0) for low in blocks]
    size = 2
    while size < shape[0]:
        mask = (differing >= size) & (differing < 2 * size)
        parts = [split(inverse) for inverse in inverses]
        offs = [split(jnp.where(mask, low, 0.0)) for low in blocks]
        firsts = [split(mm3(part, off)) for part, off in zip(parts, offs)]
        inverses = [inv - mm3(first, part) for inv, first, part in zip(inverses, firsts, parts)]
        size *= 2
    return inverses


def pick_column(array, head):
    return jnp.sum(jnp.where(iota(array.shape, 1) == head, array, 0.0), axis=1, keepdims=True)


def row_scale(keys):
    wide = keys.astype(f32)
    return lax.rsqrt(jnp.sum(wide * wide, axis=1, keepdims=True) + NORM_EPS)


def local_transits(heads):
    lows, scales = [], []
    for keys, values, raw_col, raw_row in heads:
        inner = mm(keys, keys, 1, 1)
        rows, columns = iota(inner.shape, 0), iota(inner.shape, 1)
        squares = jnp.sum(jnp.where(rows == columns, inner, 0.0), axis=0, keepdims=True)
        r_row = lax.rsqrt(squares + NORM_EPS)
        r_col = row_scale(keys)
        b_col, b_row = 2.0 * jax.nn.sigmoid(raw_col), 2.0 * jax.nn.sigmoid(raw_row)
        lows.append(jnp.where(columns < rows, inner * (b_col * r_col) * r_row, 0.0))
        scales.append((r_col, r_row, b_col, b_row))
    blocks = []
    for low in lows:
        blocks += [low[:DIM, :DIM], low[DIM:, DIM:]]
    inverses = unit_lower_inverse(blocks)
    results = []
    for index, (keys, values, raw_col, raw_row) in enumerate(heads):
        r_col, r_row, b_col, b_row = scales[index]
        upper, lower = inverses[2 * index], inverses[2 * index + 1]
        corner = mm3(split(lower), split(mm3(split(lows[index][DIM:, :DIM]), split(upper))))
        inverse = jnp.concatenate(
            [
                jnp.concatenate([upper, jnp.zeros_like(upper)], axis=1),
                jnp.concatenate([-corner, lower], axis=1),
            ],
            axis=0,
        )
        erase = mm2(split(inverse * (b_row * r_row)), keys)
        key_back = mm2(split(inverse * r_col), keys, 0, 0)
        eye = (iota((DIM, DIM), 0) == iota((DIM, DIM), 1)).astype(f32)
        erase_scaled = split(erase * r_col)
        transit = eye - (mm(keys, erase_scaled[0], 0, 0) + mm(keys, erase_scaled[1], 0, 0))
        back_scaled = split(key_back * b_col)
        offset = mm(values, back_scaled[0], 0, 0) + mm(values, back_scaled[1], 0, 0)
        results.append((inverse, erase, key_back, transit, offset, r_row))
    return results


def local_reads(queries, keys, values, raw_col, raw_row, inverse_parts, r_row):
    r_col = row_scale(keys)
    b_col, b_row = 2.0 * jax.nn.sigmoid(raw_col), 2.0 * jax.nn.sigmoid(raw_row)
    inverse = inverse_parts[0].astype(f32) + inverse_parts[1].astype(f32)
    insert = mm2(split(inverse * b_row), values)
    scores = mm(queries, keys, 1, 1) * r_row
    frame, step = iota(scores.shape, 0), iota(scores.shape, 1)
    scores = jnp.where(step <= 2 * frame + 1, scores, 0.0)
    score_back = mm3(inverse_parts, split(scores), 0, 1)
    weighted = score_back * b_col
    reads = queries.astype(f32) - mm2(split(weighted * r_col), keys, 0, 0)
    mixed = mm2(split(weighted), values, 0, 0)
    return insert, score_back, reads, mixed


def kernel(
    q_ref, k_ref, v_ref, raw_ref, cot_ref, w_ref,
    proj_ref, gq_ref, gk_ref, gv_ref, gb_ref, gw_ref,
    bcol_ref, brow_ref, k_s, v_s, inv_s,
    wg, wf, cotg, erase_s, insert_s, kback_s, sback_s, reads_s, mixed_s, rrow_s, gm_s, y_s,
    t_send, o_send, z_send, t_recv, o_recv, z_recv,
    s_send, d_send, s_recv, d_recv, mb_send, mb_full, mb_recv, gwp, gwh, gwr, gws, gwb,
    w_ss, w_rs, wx_ss, wx_rs, e_ss, e_rs, c_ss, c_rs, t_ss, t_rs, o_ss, o_rs, z_ss, z_rs,
    s_ss, s_rs, d_ss, d_rs, m_ss, m_rs, g_ss, g_rs, b_ss, b_rs,
):
    dp, me = lax.axis_index("dp"), lax.axis_index("seq")
    x, c = dp // 2, dp % 2
    y, z = me // SIDE, me % SIDE
    twin = x * 2 + (1 - c)

    def x_peer(step):
        return ((x + step) % SIDE) * 2 + c, me

    barrier = pltpu.get_barrier_semaphore()
    for step in range(1, SEQ):
        pl.semaphore_signal(barrier, inc=1, device_id=(dp, (me + step) % SEQ), device_id_type=MESH)
    for step in range(1, SIDE):
        pl.semaphore_signal(barrier, inc=1, device_id=x_peer(step), device_id_type=MESH)
    pl.semaphore_signal(barrier, inc=1, device_id=(twin, me), device_id_type=MESH)

    expand = (iota((STEPS, FRAMES), 0) // 2 == iota((STEPS, FRAMES), 1)).astype(bf16)
    raw_parts = thirds(raw_ref[...])
    columns = sum(mm(expand, part, 1, 1) for part in raw_parts)
    bcol_ref[...] = jnp.where(
        iota((STEPS, HEADS), 0) % 2 == 0, columns[:, :HEADS], columns[:, HEADS:]
    )
    rows = sum(mm(part, expand, 1, 1) for part in raw_parts)
    rows = jnp.where(iota((HEADS, STEPS), 1) % 2 == 0, rows[:HEADS], rows[HEADS:])
    for head in range(HEADS):
        brow_ref[head] = rows[head : head + 1]
    w_wide = w_ref[...].astype(f32)
    w_halves = jnp.concatenate([w_wide[:, : MODEL // 2], w_wide[:, MODEL // 2 :]], axis=0)
    wg[x, c, me] = w_halves.astype(bf16)
    cotg[x] = cot_ref[...]

    pl.semaphore_wait(barrier, SEQ - 1 + SIDE - 1 + 1)

    def remote(source, target, send_sem, recv_sem, device):
        return pltpu.make_async_remote_copy(
            src_ref=source, dst_ref=target, send_sem=send_sem, recv_sem=recv_sem,
            device_id=device, device_id_type=MESH,
        )

    def arrival(target, send_sem, recv_sem):
        remote(target, target, send_sem, recv_sem, (twin, me)).wait_recv()

    def w_copy(to):
        return remote(wg.at[x, c, me], wg.at[x, c, me], w_ss.at[to], w_rs.at[me], (dp, to))

    for step in range(1, SEQ):
        w_copy((me + step) % SEQ).start()

    before, after, across = (x + 3) % SIDE, (x + 1) % SIDE, (x + 2) % SIDE

    class Ring:
        def __init__(self, block, send_sems, recv_sems):
            self.block, self.send_sems, self.recv_sems = block, send_sems, recv_sems

        def copy(self, place, half, sem):
            ref = self.block(place, half)
            device = x_peer(1) if sem < 3 else x_peer(3)
            return remote(ref, ref, self.send_sems.at[sem], self.recv_sems.at[sem], device)

        def arrive(self, place, half, sem):
            arrival(self.block(place, half), self.send_sems.at[sem], self.recv_sems.at[sem])

        def start(self):
            for half in range(2):
                self.copy(x, half, half).start()
                self.copy(x, 1 - half, 3 + 1 - half).start()

        def relay(self):
            self.arrive(before, 0, 0)
            self.copy(before, 0, 2).start()
            self.arrive(after, 1, 4)
            self.copy(after, 1, 5).start()

        def near(self):
            self.arrive(before, 1, 1)
            self.arrive(after, 0, 3)

        def far(self):
            self.arrive(across, 0, 2)
            self.arrive(across, 1, 5)

        def sent(self):
            for half in range(2):
                self.copy(x, half, half).wait_send()
                self.copy(x, half, 3 + half).wait_send()
            self.copy(before, 0, 2).wait_send()
            self.copy(after, 1, 5).wait_send()

    w_ring = Ring(lambda place, half: wg.at[place, c, pl.ds(8 * half, 8)], wx_ss, wx_rs)
    cot_ring = Ring(lambda place, half: cotg.at[place, pl.ds(HALF * half, HALF)], c_ss, c_rs)
    places = (x, before, after, across)
    cot_ring.start()

    def core_copy(index):
        ref = wg.at[places[index], c]
        return remote(ref, ref, e_ss.at[index], e_rs.at[index], (twin, me))

    def head_lanes(head):
        return pl.ds(pl.multiple_of(head * DIM, DIM), DIM)

    def state_copies(head, half):
        owner = 2 * head + half
        rows = pl.ds(half * HALF, HALF)
        return (
            remote(t_send.at[head], t_recv.at[me], t_ss.at[owner], t_rs.at[me], (dp, owner)),
            remote(o_send.at[head, rows], o_recv.at[me], o_ss.at[owner], o_rs.at[me], (dp, owner)),
        )

    def adjoint_copy(head, half):
        owner = 2 * head + half
        rows = pl.ds(half * HALF, HALF)
        return remote(z_send.at[head, rows], z_recv.at[me], z_ss.at[owner], z_rs.at[me], (dp, owner))

    def transit_pair(index, carry):
        pair = (index + y) % SIDE
        heads = []
        for inner in range(2):
            head = 2 * pair + inner
            keys = k_ref[:, :, head_lanes(head)].reshape(STEPS, DIM)
            values = v_ref[:, :, head_lanes(head)].reshape(STEPS, DIM)
            k_s[head], v_s[head] = keys, values
            heads.append((keys, values, pick_column(bcol_ref[...], head), brow_ref[head]))
        for inner, result in enumerate(local_transits(heads)):
            head = 2 * pair + inner
            inverse, erase, key_back, transit, offset, r_row = result
            offset = offset.astype(bf16)
            t_send[head] = transit
            o_send[head] = offset
            for half in range(2):
                owner = 2 * head + half

                @pl.when(owner != me)
                def _():
                    for copy in state_copies(head, half):
                        copy.start()

                @pl.when(owner == me)
                def _():
                    t_recv[me] = transit
                    o_recv[me] = offset[half * HALF : (half + 1) * HALF]

            inv_s[0, head], inv_s[1, head] = split(inverse)
            erase_s[0, head], erase_s[1, head] = split(erase)
            kback_s[0, head], kback_s[1, head] = split(key_back)
            rrow_s[head] = r_row
        advance(index)
        return carry

    def reads_pair(index, carry):
        for inner in range(2):
            head = 2 * index + inner
            insert, score_back, reads, mixed = local_reads(
                q_ref[:, head_lanes(head)], k_s[head], v_s[head],
                pick_column(bcol_ref[...], head), brow_ref[head],
                (inv_s[0, head], inv_s[1, head]), rrow_s[head],
            )
            insert_s[head] = insert
            sback_s[0, head], sback_s[1, head] = split(score_back)
            reads_s[head] = reads.astype(bf16)
            mixed_s[head] = mixed
        advance(index + HEADS // 2)
        return carry

    def advance(index):
        @pl.when(index == W_AT)
        def _():
            for step in range(1, SEQ):
                source = (me + step) % SEQ
                arrival(wg.at[x, c, source], w_ss.at[source], w_rs.at[source])
            w_ring.start()
            core_copy(0).start()

        @pl.when(index == RELAY_AT)
        def _():
            w_ring.relay()
            w_ring.near()
            core_copy(1).start()
            core_copy(2).start()

    lax.fori_loop(0, HEADS // 2, transit_pair, 0)
    lax.fori_loop(0, HEADS // 2, reads_pair, 0)
    if FAR_FIRST:
        w_ring.far()
        core_copy(3).start()

    for step in range(1, SEQ):
        source = (me + step) % SEQ
        arrival(t_recv.at[source], t_ss.at[source], t_rs.at[source])
        arrival(o_recv.at[source], o_ss.at[source], o_rs.at[source])

    def send_state(buffer, target, value, segment, send_sems, recv_sems):
        buffer[segment] = value.astype(bf16)

        @pl.when(segment != me)
        def _():
            remote(
                buffer.at[segment], target.at[me], send_sems.at[segment], recv_sems.at[me], (dp, segment)
            ).start()

        @pl.when(segment == me)
        def _():
            target[me] = value.astype(bf16)

    def carry_state(segment, state):
        send_state(s_send, s_recv, state, segment, s_ss, s_rs)
        return mm3(split(state), split(t_recv[segment]), 1, 1) + o_recv[segment].astype(f32)

    empty = jnp.zeros((HALF, DIM), f32)
    last_state = lax.fori_loop(0, SEQ - 1, carry_state, empty)
    send_state(s_send, s_recv, last_state, SEQ - 1, s_ss, s_rs)

    if not FAR_FIRST:
        w_ring.far()
        core_copy(3).start()
    if RELAY_SPOT == 0:
        cot_ring.relay()


    def order_rows(place, core):
        def one(index, carry):
            first = wg[place, core, 2 * index].astype(f32)
            second = wg[place, core, 2 * index + 1].astype(f32)
            start = pl.multiple_of(((place * 2 + core) * 8 + index) * 16, 16)
            top = jnp.concatenate([first[:8], second[:8]], axis=0)
            bottom = jnp.concatenate([first[8:], second[8:]], axis=0)
            wf[pl.ds(start, 16), pl.ds(0, MODEL // 2)] = top.astype(bf16)
            wf[pl.ds(start, 16), pl.ds(MODEL // 2, MODEL // 2)] = bottom.astype(bf16)
            return carry

        lax.fori_loop(0, 8, one, 0, unroll=2)

    for place in places:
        order_rows(place, c)
    for index, place in enumerate(places):
        arrival(wg.at[place, 1 - c], e_ss.at[index], e_rs.at[index])
        order_rows(place, 1 - c)

    def gradient_pair(index, carry):
        pair = (index + y) % SIDE
        rows = wf[pl.ds(pl.multiple_of(pair * 2 * DIM, 2 * DIM), 2 * DIM), :]
        both = mm(cot_ref[...], rows, 1, 1).astype(bf16)
        for inner in range(2):
            head = 2 * pair + inner
            grad = both[:, inner * DIM : (inner + 1) * DIM]
            gm_s[head] = grad
            adjoint = mm(grad, reads_s[head], 0, 0).astype(bf16)
            z_send[head] = adjoint
            for half in range(2):
                owner = 2 * head + half

                @pl.when(owner != me)
                def _():
                    adjoint_copy(head, half).start()

                @pl.when(owner == me)
                def _():
                    z_recv[me] = adjoint[half * HALF : (half + 1) * HALF]

        return carry

    lax.fori_loop(0, HEADS // 2, gradient_pair, 0)

    def early_gradient(head, carry):
        y_s[head] = mm2((sback_s[0, head], sback_s[1, head]), gm_s[head])
        return carry

    lax.fori_loop(0, HEADS, early_gradient, 0)


    for step in range(1, SEQ):
        source = (me + step) % SEQ
        arrival(s_recv.at[source], s_ss.at[source], s_rs.at[source])

    def head_state(buffer, head):
        return jnp.concatenate([buffer[2 * head], buffer[2 * head + 1]], axis=0)

    def mix_head(head, carry):
        mixed = (mm(reads_s[head], head_state(s_recv, head), 1, 1) + mixed_s[head]).astype(bf16)
        mb_send[head] = mixed
        mb_full[:, head_lanes(head)] = mixed
        return carry

    lax.fori_loop(0, HEADS, mix_head, 0)

    def mixed_copy(step):
        to = (x + step) % SIDE
        return remote(
            mb_send.at[pl.ds(2 * to, 2)], mb_recv.at[:, x], m_ss.at[step - 1], m_rs.at[step - 1], x_peer(step)
        )

    for step in range(1, SIDE):
        mixed_copy(step).start()
    mb_recv[0, x] = mb_send[2 * x]
    mb_recv[1, x] = mb_send[2 * x + 1]

    for step in range(1, SEQ):
        source = (me + step) % SEQ
        arrival(z_recv.at[source], z_ss.at[source], z_rs.at[source])

    def carry_adjoint(index, adjoint):
        segment = SEQ - 1 - index
        send_state(d_send, d_recv, adjoint, segment, d_ss, d_rs)
        return mm3(split(adjoint), split(t_recv[segment])) + z_recv[segment].astype(f32)

    first_adjoint = lax.fori_loop(0, SEQ - 1, carry_adjoint, empty)
    send_state(d_send, d_recv, first_adjoint, 0, d_ss, d_rs)

    def project(index, carry):
        lanes = pl.ds(pl.multiple_of(index * COLS, COLS), COLS)
        proj_ref[:, lanes] = mm(mb_full[...], wf[:, lanes]).astype(bf16)
        return carry

    lax.fori_loop(0, MODEL // COLS, project, 0)

    def weight_chunk(inner, chunk):
        mixed = mb_recv[inner].reshape(SIDE * FRAMES, DIM)
        lanes = pl.ds(chunk * COLS, COLS)
        return lanes, mm(mixed, cotg[:, :, lanes].reshape(SIDE * FRAMES, COLS), 0, 0)

    def weight_copy(chunk):
        lanes = pl.ds(chunk * COLS, COLS)
        return remote(
            gwh.at[:, lanes], gwr.at[:, lanes], g_ss.at[chunk], g_rs.at[chunk], (twin, me)
        )

    def weight_parts():
        cot_ring.near()
        cot_ring.far()
        for step in range(1, SIDE):
            source = (x - step + SIDE) % SIDE
            arrival(mb_recv.at[:, source], m_ss.at[step - 1], m_rs.at[step - 1])
        for chunk in range(MODEL // COLS):
            lanes, part = weight_chunk(1 - c, chunk)
            gwh[:, lanes] = part.astype(bf16)
            weight_copy(chunk).start()
        for chunk in range(MODEL // COLS):
            lanes, part = weight_chunk(c, chunk)
            gwp[:, lanes] = part

    if WEIGHT_AT < 0:
        weight_parts()

    for step in range(1, SEQ):
        source = (me + step) % SEQ
        arrival(d_recv.at[source], d_ss.at[source], d_rs.at[source])

    def block_copy(step):
        to = (me + step) % SEQ
        return remote(gws.at[to], gwb.at[me], b_ss.at[to], b_rs.at[me], (dp, to))

    def backward_head(head, raw_all):
        queries, keys = q_ref[:, head_lanes(head)], k_s[head]
        raw = pick_column(raw_all, head)
        b_col = 2.0 * jax.nn.sigmoid(raw)
        r_col, r_row = row_scale(keys), rrow_s[head]
        state, later = head_state(s_recv, head), head_state(d_recv, head)
        grad = gm_s[head]
        delta = insert_s[head] - mm2((erase_s[0, head], erase_s[1, head]), state, 1, 1)
        solved = y_s[head] + mm2((kback_s[0, head], kback_s[1, head]), later, 1, 1)
        scaled = b_col * solved
        gv_ref[:, :, head_lanes(head)] = scaled.astype(bf16).reshape(FRAMES, 2, DIM)
        raw_grad = jnp.sum(solved * delta, axis=1, keepdims=True) * jax.nn.sigmoid(-raw)
        delta_parts, scaled_parts = split(delta), split(-scaled)
        score_grad = mm(grad, delta_parts[0], 1, 1) + mm(grad, delta_parts[1], 1, 1)
        frame, step = iota(score_grad.shape, 0), iota(score_grad.shape, 1)
        score_grad = jnp.where(step <= 2 * frame + 1, score_grad, 0.0)
        inner_grad = mm3(scaled_parts, delta_parts, 1, 1)
        row, column = iota(inner_grad.shape, 0), iota(inner_grad.shape, 1)
        inner_grad = jnp.where(column < row, inner_grad, 0.0)
        query_grad = mm(grad, state) + mm((score_grad * r_row).astype(bf16), keys)
        gq_ref[:, head_lanes(head)] = query_grad.astype(bf16)
        key_grad = mm(scaled_parts[0], state) + mm(delta_parts[0], later)
        key_grad = key_grad + mm(score_grad.astype(bf16), queries, 0, 0)
        key_grad = key_grad + mm((inner_grad * r_row).astype(bf16), keys)
        key_grad = key_grad + mm((inner_grad * r_col).astype(bf16), keys, 0, 0)
        unit = keys.astype(f32) * r_col
        along = jnp.sum(key_grad * unit, axis=1, keepdims=True)
        key_grad = (r_col * (key_grad - unit * along)).astype(bf16)
        gk_ref[:, :, head_lanes(head)] = key_grad.reshape(FRAMES, 2, DIM)
        return raw_grad

    lane = iota((STEPS, HEADS), 1)

    def backward_pair(index, total):
        raw_all = bcol_ref[...]
        for inner in range(2):
            head = 2 * index + inner
            total = total + jnp.where(lane == head, backward_head(head, raw_all), 0.0)

        @pl.when(index == WEIGHT_AT)
        def _():
            weight_parts()

        @pl.when(index == BLOCK_AT)
        def _():
            for chunk in range(MODEL // COLS):
                lanes = pl.ds(chunk * COLS, COLS)
                arrival(gwr.at[:, lanes], g_ss.at[chunk], g_rs.at[chunk])

            def one(index, carry):
                rows = pl.ds(pl.multiple_of(index * 16, 16), 16)
                block = gwp[rows] + gwr[rows].astype(f32)
                for inner in range(2):
                    part = block[8 * inner : 8 * inner + 8]
                    halves = [part[:, : MODEL // 2], part[:, MODEL // 2 :]]
                    gws[2 * index + inner] = jnp.concatenate(halves, axis=0).astype(bf16)
                return carry

            lax.fori_loop(0, SEQ // 2, one, 0)
            for step in range(1, SEQ):
                block_copy(step).start()
            gwb[me] = gws[me]

        return total

    raw_grad = lax.fori_loop(0, HEADS // 2, backward_pair, jnp.zeros((STEPS, HEADS), f32))
    raw_parts = thirds(raw_grad)
    for inner in range(2):
        chosen = 2 * iota((FRAMES, STEPS), 0) + inner == iota((FRAMES, STEPS), 1)
        chosen = chosen.astype(bf16)
        gb_ref[inner * HEADS : (inner + 1) * HEADS] = sum(mm(part, chosen, 0, 1) for part in raw_parts)

    for step in range(1, SEQ):
        source = (me + step) % SEQ
        arrival(gwb.at[source], b_ss.at[source], b_rs.at[source])
    total = gwb[0].astype(f32)
    for block in range(1, SEQ):
        total = total + gwb[block].astype(f32)
    gw_ref[:, : MODEL // 2] = total[:8]
    gw_ref[:, MODEL // 2 :] = total[8:]

    w_ring.sent()
    cot_ring.sent()
    for index in range(4):
        core_copy(index).wait_send()
        weight_copy(index).wait_send()
    for step in range(1, SIDE):
        mixed_copy(step).wait_send()
    for step in range(1, SEQ):
        other = (me + step) % SEQ
        block_copy(step).wait_send()
        w_copy(other).wait_send()
        remote(t_send.at[other // 2], t_recv.at[me], t_ss.at[other], t_rs.at[me], (dp, other)).wait_send()
        half_rows = pl.ds(pl.multiple_of((other % 2) * HALF, HALF), HALF)
        remote(
            o_send.at[other // 2, half_rows], o_recv.at[me], o_ss.at[other], o_rs.at[me], (dp, other)
        ).wait_send()
        remote(
            z_send.at[other // 2, half_rows], z_recv.at[me], z_ss.at[other], z_rs.at[me], (dp, other)
        ).wait_send()
        remote(s_send.at[other], s_recv.at[me], s_ss.at[other], s_rs.at[me], (dp, other)).wait_send()
        remote(d_send.at[other], d_recv.at[me], d_ss.at[other], d_rs.at[me], (dp, other)).wait_send()


def per_device(queries, key_vectors, values, beta_raw, cotangent, w_out):
    vmem = pl.BlockSpec(memory_space=pltpu.VMEM)
    dma = pltpu.SemaphoreType.DMA
    out = pl.pallas_call(
        kernel,
        out_shape=(
            jax.ShapeDtypeStruct((FRAMES, MODEL), bf16),
            jax.ShapeDtypeStruct((FRAMES, FEATURES), bf16),
            jax.ShapeDtypeStruct((FRAMES, 2, FEATURES), bf16),
            jax.ShapeDtypeStruct((FRAMES, 2, FEATURES), bf16),
            jax.ShapeDtypeStruct((2 * HEADS, FRAMES), f32),
            jax.ShapeDtypeStruct((8, MODEL), f32),
        ),
        in_specs=[vmem] * 6,
        out_specs=[vmem] * 6,
        scratch_shapes=[
            pltpu.VMEM((STEPS, HEADS), f32),
            pltpu.VMEM((HEADS, 1, STEPS), f32),
            pltpu.VMEM((HEADS, STEPS, DIM), bf16),
            pltpu.VMEM((HEADS, STEPS, DIM), bf16),
            pltpu.VMEM((2, HEADS, STEPS, STEPS), bf16),
            pltpu.VMEM((SIDE, 2, SEQ, 16, MODEL // 2), bf16),
            pltpu.VMEM((FEATURES, MODEL), bf16),
            pltpu.VMEM((SIDE, FRAMES, MODEL), bf16),
            pltpu.VMEM((2, HEADS, STEPS, DIM), bf16),
            pltpu.VMEM((HEADS, STEPS, DIM), f32),
            pltpu.VMEM((2, HEADS, STEPS, DIM), bf16),
            pltpu.VMEM((2, HEADS, STEPS, DIM), bf16),
            pltpu.VMEM((HEADS, FRAMES, DIM), bf16),
            pltpu.VMEM((HEADS, FRAMES, DIM), f32),
            pltpu.VMEM((HEADS, 1, STEPS), f32),
            pltpu.VMEM((HEADS, FRAMES, DIM), bf16),
            pltpu.VMEM((HEADS, STEPS, DIM), f32),
            pltpu.VMEM((HEADS, DIM, DIM), f32),
            pltpu.VMEM((HEADS, DIM, DIM), bf16),
            pltpu.VMEM((HEADS, DIM, DIM), bf16),
            pltpu.VMEM((SEQ, DIM, DIM), f32),
            pltpu.VMEM((SEQ, HALF, DIM), bf16),
            pltpu.VMEM((SEQ, HALF, DIM), bf16),
            pltpu.VMEM((SEQ, HALF, DIM), bf16),
            pltpu.VMEM((SEQ, HALF, DIM), bf16),
            pltpu.VMEM((SEQ, HALF, DIM), bf16),
            pltpu.VMEM((SEQ, HALF, DIM), bf16),
            pltpu.VMEM((HEADS, FRAMES, DIM), bf16),
            pltpu.VMEM((FRAMES, FEATURES), bf16),
            pltpu.VMEM((2, SIDE, FRAMES, DIM), bf16),
            pltpu.VMEM((DIM, MODEL), f32),
            pltpu.VMEM((DIM, MODEL), bf16),
            pltpu.VMEM((DIM, MODEL), bf16),
            pltpu.VMEM((SEQ, 16, MODEL // 2), bf16),
            pltpu.VMEM((SEQ, 16, MODEL // 2), bf16),
            dma((SEQ,)), dma((SEQ,)), dma((6,)), dma((6,)), dma((4,)), dma((4,)), dma((6,)), dma((6,)),
            dma((SEQ,)), dma((SEQ,)), dma((SEQ,)), dma((SEQ,)), dma((SEQ,)), dma((SEQ,)),
            dma((SEQ,)), dma((SEQ,)), dma((SEQ,)), dma((SEQ,)),
            dma((3,)), dma((3,)), dma((4,)), dma((4,)), dma((SEQ,)), dma((SEQ,)),
        ],
        compiler_params=pltpu.CompilerParams(
            collective_id=0, has_side_effects=True, vmem_limit_bytes=60 * 1024 * 1024
        ),
        name="delta_product",
    )(
        queries[0],
        key_vectors[0],
        values[0],
        beta_raw[0].T,
        cotangent[0],
        w_out,
    )
    projected, grad_query, grad_key, grad_value, grad_raw, grad_weight = out
    return (
        projected[None],
        grad_query[None],
        grad_key[None],
        grad_value[None],
        grad_raw.T[None],
        grad_weight,
    )


def solution(mesh):
    in_specs = (
        P("dp", "seq", None),
        P("dp", "seq", None, None),
        P("dp", "seq", None, None),
        P("dp", "seq", None),
        P("dp", "seq", None),
        P(("dp", "seq"), None),
    )
    out_specs = (
        P("dp", "seq", None),
        P("dp", "seq", None),
        P("dp", "seq", None, None),
        P("dp", "seq", None, None),
        P("dp", "seq", None),
        P(("dp", "seq"), None),
    )
    return jax.shard_map(
        per_device, mesh=mesh, in_specs=in_specs, out_specs=out_specs, check_vma=False
    )
```

```python
import jax
import jax.numpy as jnp
from jax import lax
from jax.experimental import pallas as pl
from jax.experimental.pallas import tpu as pltpu
from jax.sharding import PartitionSpec as P

f32, bf16 = jnp.float32, jnp.bfloat16
MESH = pl.DeviceIdType.MESH
NORM_EPS = 1e-06
HEADS = 8
DIM = 128
HALF = 64
FRAMES = 128
STEPS = 256
MODEL = 2048
FEATURES = HEADS * DIM
SEQ = 16
SIDE = 4
COLS = 512
W_AT = 1
RELAY_AT = 5
WEIGHT_AT = -1
BLOCK_AT = -1
FAR_FIRST = 1
RELAY_SPOT = 0
PROJECT_FIRST = 0


def mm(a, b, ca=1, cb=0):
    return lax.dot_general(a, b, (((ca,), (cb,)), ((), ())), preferred_element_type=f32)


def split(x):
    high = x.astype(bf16)
    return high, (x - high.astype(f32)).astype(bf16)


def mm2(a, b, ca=1, cb=0):
    return mm(a[0], b, ca, cb) + mm(a[1], b, ca, cb)


def mm3(a, b, ca=1, cb=0):
    return mm(a[0], b[0], ca, cb) + (mm(a[0], b[1], ca, cb) + mm(a[1], b[0], ca, cb))


def thirds(x):
    high = x.astype(bf16)
    rest = x - high.astype(f32)
    middle = rest.astype(bf16)
    return high, middle, (rest - middle.astype(f32)).astype(bf16)


def iota(shape, axis):
    return lax.broadcasted_iota(jnp.int32, shape, axis)


def unit_lower_inverse(blocks):
    shape = blocks[0].shape
    rows, columns = iota(shape, 0), iota(shape, 1)
    differing = rows ^ columns
    eye = (rows == columns).astype(f32)
    inverses = [eye - jnp.where(differing == 1, low, 0.0) for low in blocks]
    size = 2
    while size < shape[0]:
        mask = (differing >= size) & (differing < 2 * size)
        parts = [split(inverse) for inverse in inverses]
        offs = [split(jnp.where(mask, low, 0.0)) for low in blocks]
        firsts = [split(mm3(part, off)) for part, off in zip(parts, offs)]
        inverses = [inv - mm3(first, part) for inv, first, part in zip(inverses, firsts, parts)]
        size *= 2
    return inverses


def pick_column(array, head):
    return jnp.sum(jnp.where(iota(array.shape, 1) == head, array, 0.0), axis=1, keepdims=True)


def row_scale(keys):
    wide = keys.astype(f32)
    return lax.rsqrt(jnp.sum(wide * wide, axis=1, keepdims=True) + NORM_EPS)


def local_transits(heads):
    lows, scales = [], []
    for keys, values, raw_col, raw_row in heads:
        inner = mm(keys, keys, 1, 1)
        rows, columns = iota(inner.shape, 0), iota(inner.shape, 1)
        squares = jnp.sum(jnp.where(rows == columns, inner, 0.0), axis=0, keepdims=True)
        r_row = lax.rsqrt(squares + NORM_EPS)
        r_col = row_scale(keys)
        b_col, b_row = 2.0 * jax.nn.sigmoid(raw_col), 2.0 * jax.nn.sigmoid(raw_row)
        lows.append(jnp.where(columns < rows, inner * (b_col * r_col) * r_row, 0.0))
        scales.append((r_col, r_row, b_col, b_row))
    blocks = []
    for low in lows:
        blocks += [low[:DIM, :DIM], low[DIM:, DIM:]]
    inverses = unit_lower_inverse(blocks)
    results = []
    for index, (keys, values, raw_col, raw_row) in enumerate(heads):
        r_col, r_row, b_col, b_row = scales[index]
        upper, lower = inverses[2 * index], inverses[2 * index + 1]
        corner = mm3(split(lower), split(mm3(split(lows[index][DIM:, :DIM]), split(upper))))
        inverse = jnp.concatenate(
            [
                jnp.concatenate([upper, jnp.zeros_like(upper)], axis=1),
                jnp.concatenate([-corner, lower], axis=1),
            ],
            axis=0,
        )
        erase = mm2(split(inverse * (b_row * r_row)), keys)
        key_back = mm2(split(inverse * r_col), keys, 0, 0)
        eye = (iota((DIM, DIM), 0) == iota((DIM, DIM), 1)).astype(f32)
        erase_scaled = split(erase * r_col)
        transit = eye - (mm(keys, erase_scaled[0], 0, 0) + mm(keys, erase_scaled[1], 0, 0))
        back_scaled = split(key_back * b_col)
        offset = mm(values, back_scaled[0], 0, 0) + mm(values, back_scaled[1], 0, 0)
        results.append((inverse, erase, key_back, transit, offset, r_row))
    return results


def local_reads(queries, keys, values, raw_col, raw_row, inverse_parts, r_row):
    r_col = row_scale(keys)
    b_col, b_row = 2.0 * jax.nn.sigmoid(raw_col), 2.0 * jax.nn.sigmoid(raw_row)
    inverse = inverse_parts[0].astype(f32) + inverse_parts[1].astype(f32)
    insert = mm2(split(inverse * b_row), values)
    scores = mm(queries, keys, 1, 1) * r_row
    frame, step = iota(scores.shape, 0), iota(scores.shape, 1)
    scores = jnp.where(step <= 2 * frame + 1, scores, 0.0)
    score_back = mm3(inverse_parts, split(scores), 0, 1)
    weighted = score_back * b_col
    reads = queries.astype(f32) - mm2(split(weighted * r_col), keys, 0, 0)
    mixed = mm2(split(weighted), values, 0, 0)
    return insert, score_back, reads, mixed


def kernel(
    q_ref, k_ref, v_ref, raw_ref, cot_ref, w_ref,
    proj_ref, gq_ref, gk_ref, gv_ref, gb_ref, gw_ref,
    bcol_ref, brow_ref, k_s, v_s, inv_s,
    wg, wf, cotg, erase_s, insert_s, kback_s, sback_s, reads_s, mixed_s, rrow_s, gm_s, y_s,
    t_send, o_send, z_send, t_recv, o_recv, z_recv,
    s_send, d_send, s_recv, d_recv, mb_send, mb_full, mb_recv, gwp, gwh, gwr, gws, gwb,
    w_ss, w_rs, wx_ss, wx_rs, e_ss, e_rs, c_ss, c_rs, t_ss, t_rs, o_ss, o_rs, z_ss, z_rs,
    s_ss, s_rs, d_ss, d_rs, m_ss, m_rs, g_ss, g_rs, b_ss, b_rs,
):
    dp, me = lax.axis_index("dp"), lax.axis_index("seq")
    x, c = dp // 2, dp % 2
    y, z = me // SIDE, me % SIDE
    twin = x * 2 + (1 - c)

    def x_peer(step):
        return ((x + step) % SIDE) * 2 + c, me

    barrier = pltpu.get_barrier_semaphore()
    for step in range(1, SEQ):
        pl.semaphore_signal(barrier, inc=1, device_id=(dp, (me + step) % SEQ), device_id_type=MESH)
    for step in range(1, SIDE):
        pl.semaphore_signal(barrier, inc=1, device_id=x_peer(step), device_id_type=MESH)
    pl.semaphore_signal(barrier, inc=1, device_id=(twin, me), device_id_type=MESH)

    expand = (iota((STEPS, FRAMES), 0) // 2 == iota((STEPS, FRAMES), 1)).astype(bf16)
    raw_parts = thirds(raw_ref[...])
    columns = sum(mm(expand, part, 1, 1) for part in raw_parts)
    bcol_ref[...] = jnp.where(
        iota((STEPS, HEADS), 0) % 2 == 0, columns[:, :HEADS], columns[:, HEADS:]
    )
    rows = sum(mm(part, expand, 1, 1) for part in raw_parts)
    rows = jnp.where(iota((HEADS, STEPS), 1) % 2 == 0, rows[:HEADS], rows[HEADS:])
    for head in range(HEADS):
        brow_ref[head] = rows[head : head + 1]
    w_wide = w_ref[...].astype(f32)
    w_halves = jnp.concatenate([w_wide[:, : MODEL // 2], w_wide[:, MODEL // 2 :]], axis=0)
    wg[x, c, me] = w_halves.astype(bf16)
    cotg[x] = cot_ref[...]

    pl.semaphore_wait(barrier, SEQ - 1 + SIDE - 1 + 1)

    def remote(source, target, send_sem, recv_sem, device):
        return pltpu.make_async_remote_copy(
            src_ref=source, dst_ref=target, send_sem=send_sem, recv_sem=recv_sem,
            device_id=device, device_id_type=MESH,
        )

    def arrival(target, send_sem, recv_sem):
        remote(target, target, send_sem, recv_sem, (twin, me)).wait_recv()

    def w_copy(to):
        return remote(wg.at[x, c, me], wg.at[x, c, me], w_ss.at[to], w_rs.at[me], (dp, to))

    for step in range(1, SEQ):
        w_copy((me + step) % SEQ).start()

    before, after, across = (x + 3) % SIDE, (x + 1) % SIDE, (x + 2) % SIDE

    class Ring:
        def __init__(self, block, send_sems, recv_sems):
            self.block, self.send_sems, self.recv_sems = block, send_sems, recv_sems

        def copy(self, place, half, sem):
            ref = self.block(place, half)
            device = x_peer(1) if sem < 3 else x_peer(3)
            return remote(ref, ref, self.send_sems.at[sem], self.recv_sems.at[sem], device)

        def arrive(self, place, half, sem):
            arrival(self.block(place, half), self.send_sems.at[sem], self.recv_sems.at[sem])

        def start(self):
            for half in range(2):
                self.copy(x, half, half).start()
                self.copy(x, 1 - half, 3 + 1 - half).start()

        def relay(self):
            self.arrive(before, 0, 0)
            self.copy(before, 0, 2).start()
            self.arrive(after, 1, 4)
            self.copy(after, 1, 5).start()

        def near(self):
            self.arrive(before, 1, 1)
            self.arrive(after, 0, 3)

        def far(self):
            self.arrive(across, 0, 2)
            self.arrive(across, 1, 5)

        def sent(self):
            for half in range(2):
                self.copy(x, half, half).wait_send()
                self.copy(x, half, 3 + half).wait_send()
            self.copy(before, 0, 2).wait_send()
            self.copy(after, 1, 5).wait_send()

    w_ring = Ring(lambda place, half: wg.at[place, c, pl.ds(8 * half, 8)], wx_ss, wx_rs)
    cot_ring = Ring(lambda place, half: cotg.at[place, pl.ds(HALF * half, HALF)], c_ss, c_rs)
    places = (x, before, after, across)
    cot_ring.start()

    def core_copy(index):
        ref = wg.at[places[index], c]
        return remote(ref, ref, e_ss.at[index], e_rs.at[index], (twin, me))

    def head_lanes(head):
        return pl.ds(pl.multiple_of(head * DIM, DIM), DIM)

    def state_copies(head, half):
        owner = 2 * head + half
        rows = pl.ds(half * HALF, HALF)
        return (
            remote(t_send.at[head], t_recv.at[me], t_ss.at[owner], t_rs.at[me], (dp, owner)),
            remote(o_send.at[head, rows], o_recv.at[me], o_ss.at[owner], o_rs.at[me], (dp, owner)),
        )

    def adjoint_copy(head, half):
        owner = 2 * head + half
        rows = pl.ds(half * HALF, HALF)
        return remote(z_send.at[head, rows], z_recv.at[me], z_ss.at[owner], z_rs.at[me], (dp, owner))

    def transit_pair(index, carry):
        pair = (index + y) % SIDE
        heads = []
        for inner in range(2):
            head = 2 * pair + inner
            keys = k_ref[:, :, head_lanes(head)].reshape(STEPS, DIM)
            values = v_ref[:, :, head_lanes(head)].reshape(STEPS, DIM)
            k_s[head], v_s[head] = keys, values
            heads.append((keys, values, pick_column(bcol_ref[...], head), brow_ref[head]))
        for inner, result in enumerate(local_transits(heads)):
            head = 2 * pair + inner
            inverse, erase, key_back, transit, offset, r_row = result
            offset = offset.astype(bf16)
            t_send[head] = transit
            o_send[head] = offset
            for half in range(2):
                owner = 2 * head + half

                @pl.when(owner != me)
                def _():
                    for copy in state_copies(head, half):
                        copy.start()

                @pl.when(owner == me)
                def _():
                    t_recv[me] = transit
                    o_recv[me] = offset[half * HALF : (half + 1) * HALF]

            inv_s[0, head], inv_s[1, head] = split(inverse)
            erase_s[0, head], erase_s[1, head] = split(erase)
            kback_s[0, head], kback_s[1, head] = split(key_back)
            rrow_s[head] = r_row
        advance(index)
        return carry

    def reads_pair(index, carry):
        for inner in range(2):
            head = 2 * index + inner
            insert, score_back, reads, mixed = local_reads(
                q_ref[:, head_lanes(head)], k_s[head], v_s[head],
                pick_column(bcol_ref[...], head), brow_ref[head],
                (inv_s[0, head], inv_s[1, head]), rrow_s[head],
            )
            insert_s[head] = insert
            sback_s[0, head], sback_s[1, head] = split(score_back)
            reads_s[head] = reads.astype(bf16)
            mixed_s[head] = mixed
        advance(index + HEADS // 2)
        return carry

    def advance(index):
        @pl.when(index == W_AT)
        def _():
            for step in range(1, SEQ):
                source = (me + step) % SEQ
                arrival(wg.at[x, c, source], w_ss.at[source], w_rs.at[source])
            w_ring.start()
            core_copy(0).start()

        @pl.when(index == RELAY_AT)
        def _():
            w_ring.relay()
            w_ring.near()
            core_copy(1).start()
            core_copy(2).start()

    lax.fori_loop(0, HEADS // 2, transit_pair, 0)
    lax.fori_loop(0, HEADS // 2, reads_pair, 0)
    if FAR_FIRST:
        w_ring.far()
        core_copy(3).start()

    for step in range(1, SEQ):
        source = (me + step) % SEQ
        arrival(t_recv.at[source], t_ss.at[source], t_rs.at[source])
        arrival(o_recv.at[source], o_ss.at[source], o_rs.at[source])

    def send_state(buffer, target, value, segment, send_sems, recv_sems):
        buffer[segment] = value.astype(bf16)

        @pl.when(segment != me)
        def _():
            remote(
                buffer.at[segment], target.at[me], send_sems.at[segment], recv_sems.at[me], (dp, segment)
            ).start()

        @pl.when(segment == me)
        def _():
            target[me] = value.astype(bf16)

    def carry_state(segment, state):
        send_state(s_send, s_recv, state, segment, s_ss, s_rs)
        return mm3(split(state), split(t_recv[segment]), 1, 1) + o_recv[segment].astype(f32)

    empty = jnp.zeros((HALF, DIM), f32)
    last_state = lax.fori_loop(0, SEQ - 1, carry_state, empty)
    send_state(s_send, s_recv, last_state, SEQ - 1, s_ss, s_rs)

    if not FAR_FIRST:
        w_ring.far()
        core_copy(3).start()
    if RELAY_SPOT == 0:
        cot_ring.relay()


    def order_rows(place, core):
        def one(index, carry):
            first = wg[place, core, 2 * index].astype(f32)
            second = wg[place, core, 2 * index + 1].astype(f32)
            start = pl.multiple_of(((place * 2 + core) * 8 + index) * 16, 16)
            top = jnp.concatenate([first[:8], second[:8]], axis=0)
            bottom = jnp.concatenate([first[8:], second[8:]], axis=0)
            wf[pl.ds(start, 16), pl.ds(0, MODEL // 2)] = top.astype(bf16)
            wf[pl.ds(start, 16), pl.ds(MODEL // 2, MODEL // 2)] = bottom.astype(bf16)
            return carry

        lax.fori_loop(0, 8, one, 0, unroll=2)

    for place in places:
        order_rows(place, c)
    for index, place in enumerate(places):
        arrival(wg.at[place, 1 - c], e_ss.at[index], e_rs.at[index])
        order_rows(place, 1 - c)

    def gradient_pair(index, carry):
        pair = (index + y) % SIDE
        rows = wf[pl.ds(pl.multiple_of(pair * 2 * DIM, 2 * DIM), 2 * DIM), :]
        both = mm(cot_ref[...], rows, 1, 1).astype(bf16)
        for inner in range(2):
            head = 2 * pair + inner
            grad = both[:, inner * DIM : (inner + 1) * DIM]
            gm_s[head] = grad
            adjoint = mm(grad, reads_s[head], 0, 0).astype(bf16)
            z_send[head] = adjoint
            for half in range(2):
                owner = 2 * head + half

                @pl.when(owner != me)
                def _():
                    adjoint_copy(head, half).start()

                @pl.when(owner == me)
                def _():
                    z_recv[me] = adjoint[half * HALF : (half + 1) * HALF]

        return carry

    lax.fori_loop(0, HEADS // 2, gradient_pair, 0)

    for step in range(1, SEQ):
        source = (me + step) % SEQ
        arrival(s_recv.at[source], s_ss.at[source], s_rs.at[source])

    def head_state(buffer, head):
        return jnp.concatenate([buffer[2 * head], buffer[2 * head + 1]], axis=0)

    def mix_head(head, carry):
        mixed = (mm(reads_s[head], head_state(s_recv, head), 1, 1) + mixed_s[head]).astype(bf16)
        mb_send[head] = mixed
        mb_full[:, head_lanes(head)] = mixed
        return carry

    lax.fori_loop(0, HEADS, mix_head, 0)

    def mixed_copy(step):
        to = (x + step) % SIDE
        return remote(
            mb_send.at[pl.ds(2 * to, 2)], mb_recv.at[:, x], m_ss.at[step - 1], m_rs.at[step - 1], x_peer(step)
        )

    for step in range(1, SIDE):
        mixed_copy(step).start()
    mb_recv[0, x] = mb_send[2 * x]
    mb_recv[1, x] = mb_send[2 * x + 1]

    def early_gradient(head, carry):
        y_s[head] = mm2((sback_s[0, head], sback_s[1, head]), gm_s[head])
        return carry

    lax.fori_loop(0, HEADS, early_gradient, 0)

    for step in range(1, SEQ):
        source = (me + step) % SEQ
        arrival(z_recv.at[source], z_ss.at[source], z_rs.at[source])

    def carry_adjoint(index, adjoint):
        segment = SEQ - 1 - index
        send_state(d_send, d_recv, adjoint, segment, d_ss, d_rs)
        return mm3(split(adjoint), split(t_recv[segment])) + z_recv[segment].astype(f32)

    first_adjoint = lax.fori_loop(0, SEQ - 1, carry_adjoint, empty)
    send_state(d_send, d_recv, first_adjoint, 0, d_ss, d_rs)

    def project(index, carry):
        lanes = pl.ds(pl.multiple_of(index * COLS, COLS), COLS)
        proj_ref[:, lanes] = mm(mb_full[...], wf[:, lanes]).astype(bf16)
        return carry

    if PROJECT_FIRST:
        lax.fori_loop(0, MODEL // COLS, project, 0)

    def weight_chunk(inner, chunk):
        mixed = mb_recv[inner].reshape(SIDE * FRAMES, DIM)
        lanes = pl.ds(chunk * COLS, COLS)
        return lanes, mm(mixed, cotg[:, :, lanes].reshape(SIDE * FRAMES, COLS), 0, 0)

    def weight_copy(chunk):
        lanes = pl.ds(chunk * COLS, COLS)
        return remote(
            gwh.at[:, lanes], gwr.at[:, lanes], g_ss.at[chunk], g_rs.at[chunk], (twin, me)
        )

    def weight_parts():
        cot_ring.near()
        cot_ring.far()
        for step in range(1, SIDE):
            source = (x - step + SIDE) % SIDE
            arrival(mb_recv.at[:, source], m_ss.at[step - 1], m_rs.at[step - 1])
        for chunk in range(MODEL // COLS):
            lanes, part = weight_chunk(1 - c, chunk)
            gwh[:, lanes] = part.astype(bf16)
            weight_copy(chunk).start()
        for chunk in range(MODEL // COLS):
            lanes, part = weight_chunk(c, chunk)
            gwp[:, lanes] = part

    if WEIGHT_AT < 0:
        weight_parts()


    def block_copy(step):
        to = (me + step) % SEQ
        return remote(gws.at[to], gwb.at[me], b_ss.at[to], b_rs.at[me], (dp, to))

    def send_blocks():
        for chunk in range(MODEL // COLS):
            lanes = pl.ds(chunk * COLS, COLS)
            arrival(gwr.at[:, lanes], g_ss.at[chunk], g_rs.at[chunk])

        def one(index, carry):
            rows = pl.ds(pl.multiple_of(index * 16, 16), 16)
            block = gwp[rows] + gwr[rows].astype(f32)
            for inner in range(2):
                part = block[8 * inner : 8 * inner + 8]
                halves = [part[:, : MODEL // 2], part[:, MODEL // 2 :]]
                gws[2 * index + inner] = jnp.concatenate(halves, axis=0).astype(bf16)
            return carry

        lax.fori_loop(0, SEQ // 2, one, 0)
        for step in range(1, SEQ):
            block_copy(step).start()
        gwb[me] = gws[me]

    def backward_head(head, raw_all):
        queries, keys = q_ref[:, head_lanes(head)], k_s[head]
        raw = pick_column(raw_all, head)
        b_col = 2.0 * jax.nn.sigmoid(raw)
        r_col, r_row = row_scale(keys), rrow_s[head]
        state, later = head_state(s_recv, head), head_state(d_recv, head)
        grad = gm_s[head]
        delta = insert_s[head] - mm2((erase_s[0, head], erase_s[1, head]), state, 1, 1)
        solved = y_s[head] + mm2((kback_s[0, head], kback_s[1, head]), later, 1, 1)
        scaled = b_col * solved
        gv_ref[:, :, head_lanes(head)] = scaled.astype(bf16).reshape(FRAMES, 2, DIM)
        raw_grad = jnp.sum(solved * delta, axis=1, keepdims=True) * jax.nn.sigmoid(-raw)
        delta_parts, scaled_parts = split(delta), split(-scaled)
        score_grad = mm(grad, delta_parts[0], 1, 1) + mm(grad, delta_parts[1], 1, 1)
        frame, step = iota(score_grad.shape, 0), iota(score_grad.shape, 1)
        score_grad = jnp.where(step <= 2 * frame + 1, score_grad, 0.0)
        inner_grad = mm3(scaled_parts, delta_parts, 1, 1)
        row, column = iota(inner_grad.shape, 0), iota(inner_grad.shape, 1)
        inner_grad = jnp.where(column < row, inner_grad, 0.0)
        query_grad = mm(grad, state) + mm((score_grad * r_row).astype(bf16), keys)
        gq_ref[:, head_lanes(head)] = query_grad.astype(bf16)
        key_grad = mm(scaled_parts[0], state) + mm(delta_parts[0], later)
        key_grad = key_grad + mm(score_grad.astype(bf16), queries, 0, 0)
        key_grad = key_grad + mm((inner_grad * r_row).astype(bf16), keys)
        key_grad = key_grad + mm((inner_grad * r_col).astype(bf16), keys, 0, 0)
        unit = keys.astype(f32) * r_col
        along = jnp.sum(key_grad * unit, axis=1, keepdims=True)
        key_grad = (r_col * (key_grad - unit * along)).astype(bf16)
        gk_ref[:, :, head_lanes(head)] = key_grad.reshape(FRAMES, 2, DIM)
        return raw_grad

    if not PROJECT_FIRST:
        lax.fori_loop(0, MODEL // COLS, project, 0)
    if BLOCK_AT < 0:
        send_blocks()
    for step in range(1, SEQ):
        source = (me + step) % SEQ
        arrival(d_recv.at[source], d_ss.at[source], d_rs.at[source])

    lane = iota((STEPS, HEADS), 1)

    def backward_pair(index, total):
        raw_all = bcol_ref[...]
        for inner in range(2):
            head = 2 * index + inner
            total = total + jnp.where(lane == head, backward_head(head, raw_all), 0.0)

        @pl.when(index == WEIGHT_AT)
        def _():
            weight_parts()

        @pl.when(index == BLOCK_AT)
        def _():
            send_blocks()

        return total

    raw_grad = lax.fori_loop(0, HEADS // 2, backward_pair, jnp.zeros((STEPS, HEADS), f32))
    raw_parts = thirds(raw_grad)
    for inner in range(2):
        chosen = 2 * iota((FRAMES, STEPS), 0) + inner == iota((FRAMES, STEPS), 1)
        chosen = chosen.astype(bf16)
        gb_ref[inner * HEADS : (inner + 1) * HEADS] = sum(mm(part, chosen, 0, 1) for part in raw_parts)

    for step in range(1, SEQ):
        source = (me + step) % SEQ
        arrival(gwb.at[source], b_ss.at[source], b_rs.at[source])
    total = gwb[0].astype(f32)
    for block in range(1, SEQ):
        total = total + gwb[block].astype(f32)
    gw_ref[:, : MODEL // 2] = total[:8]
    gw_ref[:, MODEL // 2 :] = total[8:]

    w_ring.sent()
    cot_ring.sent()
    for index in range(4):
        core_copy(index).wait_send()
        weight_copy(index).wait_send()
    for step in range(1, SIDE):
        mixed_copy(step).wait_send()
    for step in range(1, SEQ):
        other = (me + step) % SEQ
        block_copy(step).wait_send()
        w_copy(other).wait_send()
        remote(t_send.at[other // 2], t_recv.at[me], t_ss.at[other], t_rs.at[me], (dp, other)).wait_send()
        half_rows = pl.ds(pl.multiple_of((other % 2) * HALF, HALF), HALF)
        remote(
            o_send.at[other // 2, half_rows], o_recv.at[me], o_ss.at[other], o_rs.at[me], (dp, other)
        ).wait_send()
        remote(
            z_send.at[other // 2, half_rows], z_recv.at[me], z_ss.at[other], z_rs.at[me], (dp, other)
        ).wait_send()
        remote(s_send.at[other], s_recv.at[me], s_ss.at[other], s_rs.at[me], (dp, other)).wait_send()
        remote(d_send.at[other], d_recv.at[me], d_ss.at[other], d_rs.at[me], (dp, other)).wait_send()


def per_device(queries, key_vectors, values, beta_raw, cotangent, w_out):
    vmem = pl.BlockSpec(memory_space=pltpu.VMEM)
    dma = pltpu.SemaphoreType.DMA
    out = pl.pallas_call(
        kernel,
        out_shape=(
            jax.ShapeDtypeStruct((FRAMES, MODEL), bf16),
            jax.ShapeDtypeStruct((FRAMES, FEATURES), bf16),
            jax.ShapeDtypeStruct((FRAMES, 2, FEATURES), bf16),
            jax.ShapeDtypeStruct((FRAMES, 2, FEATURES), bf16),
            jax.ShapeDtypeStruct((2 * HEADS, FRAMES), f32),
            jax.ShapeDtypeStruct((8, MODEL), f32),
        ),
        in_specs=[vmem] * 6,
        out_specs=[vmem] * 6,
        scratch_shapes=[
            pltpu.VMEM((STEPS, HEADS), f32),
            pltpu.VMEM((HEADS, 1, STEPS), f32),
            pltpu.VMEM((HEADS, STEPS, DIM), bf16),
            pltpu.VMEM((HEADS, STEPS, DIM), bf16),
            pltpu.VMEM((2, HEADS, STEPS, STEPS), bf16),
            pltpu.VMEM((SIDE, 2, SEQ, 16, MODEL // 2), bf16),
            pltpu.VMEM((FEATURES, MODEL), bf16),
            pltpu.VMEM((SIDE, FRAMES, MODEL), bf16),
            pltpu.VMEM((2, HEADS, STEPS, DIM), bf16),
            pltpu.VMEM((HEADS, STEPS, DIM), f32),
            pltpu.VMEM((2, HEADS, STEPS, DIM), bf16),
            pltpu.VMEM((2, HEADS, STEPS, DIM), bf16),
            pltpu.VMEM((HEADS, FRAMES, DIM), bf16),
            pltpu.VMEM((HEADS, FRAMES, DIM), f32),
            pltpu.VMEM((HEADS, 1, STEPS), f32),
            pltpu.VMEM((HEADS, FRAMES, DIM), bf16),
            pltpu.VMEM((HEADS, STEPS, DIM), f32),
            pltpu.VMEM((HEADS, DIM, DIM), f32),
            pltpu.VMEM((HEADS, DIM, DIM), bf16),
            pltpu.VMEM((HEADS, DIM, DIM), bf16),
            pltpu.VMEM((SEQ, DIM, DIM), f32),
            pltpu.VMEM((SEQ, HALF, DIM), bf16),
            pltpu.VMEM((SEQ, HALF, DIM), bf16),
            pltpu.VMEM((SEQ, HALF, DIM), bf16),
            pltpu.VMEM((SEQ, HALF, DIM), bf16),
            pltpu.VMEM((SEQ, HALF, DIM), bf16),
            pltpu.VMEM((SEQ, HALF, DIM), bf16),
            pltpu.VMEM((HEADS, FRAMES, DIM), bf16),
            pltpu.VMEM((FRAMES, FEATURES), bf16),
            pltpu.VMEM((2, SIDE, FRAMES, DIM), bf16),
            pltpu.VMEM((DIM, MODEL), f32),
            pltpu.VMEM((DIM, MODEL), bf16),
            pltpu.VMEM((DIM, MODEL), bf16),
            pltpu.VMEM((SEQ, 16, MODEL // 2), bf16),
            pltpu.VMEM((SEQ, 16, MODEL // 2), bf16),
            dma((SEQ,)), dma((SEQ,)), dma((6,)), dma((6,)), dma((4,)), dma((4,)), dma((6,)), dma((6,)),
            dma((SEQ,)), dma((SEQ,)), dma((SEQ,)), dma((SEQ,)), dma((SEQ,)), dma((SEQ,)),
            dma((SEQ,)), dma((SEQ,)), dma((SEQ,)), dma((SEQ,)),
            dma((3,)), dma((3,)), dma((4,)), dma((4,)), dma((SEQ,)), dma((SEQ,)),
        ],
        compiler_params=pltpu.CompilerParams(
            collective_id=0, has_side_effects=True, vmem_limit_bytes=60 * 1024 * 1024
        ),
        name="delta_product",
    )(
        queries[0],
        key_vectors[0],
        values[0],
        beta_raw[0].T,
        cotangent[0],
        w_out,
    )
    projected, grad_query, grad_key, grad_value, grad_raw, grad_weight = out
    return (
        projected[None],
        grad_query[None],
        grad_key[None],
        grad_value[None],
        grad_raw.T[None],
        grad_weight,
    )


def solution(mesh):
    in_specs = (
        P("dp", "seq", None),
        P("dp", "seq", None, None),
        P("dp", "seq", None, None),
        P("dp", "seq", None),
        P("dp", "seq", None),
        P(("dp", "seq"), None),
    )
    out_specs = (
        P("dp", "seq", None),
        P("dp", "seq", None),
        P("dp", "seq", None, None),
        P("dp", "seq", None, None),
        P("dp", "seq", None),
        P(("dp", "seq"), None),
    )
    return jax.shard_map(
        per_device, mesh=mesh, in_specs=in_specs, out_specs=out_specs, check_vma=False
    )
```
